32 devices in a mesh: strip: 2 (over y), col: 4 (over z), row: 4 (over x, core).
Axes of the slice: x: 2, y: 2, z: 4, core: 2. Of those that a mesh axis runs over, the one named last changes fastest.
Arguments:
- left_features: bfloat16 [64, 2048, 128], P(('strip', 'row'), 'col'), parts along dimension 0, may hold values from -6 to 6
- right_features: bfloat16 [64, 2048, 128], P(('strip', 'row'), 'col'), parts along dimension 0, may hold values from -6 to 6
- conv_first: bfloat16 [3, 3, 256, 256], replicated, may hold values from -0.125 to 0.125
- conv_second: bfloat16 [3, 3, 256, 256], replicated, may hold values from -0.125 to 0.125
Outputs:
- cost_field: bfloat16 [64, 2048, 256], P(('strip', 'row'), 'col'), parts along dimension 0
The draws below stay inside these ranges and needn't reach their ends.
There are 2 independent parts, one for each index of `strip`. The reference program is written for one: setup_inputs(seed, part) draws one part's arguments, and reference() takes and returns one part's arrays. A program takes and returns all parts, laid end to end along the dimension named above; an argument that names none is the same for every part. Nothing has to cross between parts.
All inputs are finite; a program needn't handle non-finite values.
Results may differ from the reference program's by a relative error of at most 0.0058.
Values may be sent and summed in bfloat16 or wider, within the bound.
No kernel may reach another device: no remote copies, remote signals or barrier semaphores. Data moves between devices by JAX's collectives and lax.ppermute only.
A program may use at most 128 MiB of HBM per device.

```python
import jax
import jax.numpy as jnp
from jax import lax

C = 128
DISP = 256
H = 32
W = 2048


def shard_levels(key, dims, pieces, low, high):
    gain = 1.0
    for position, shards_of in pieces:
        steps = jax.random.uniform(jax.random.fold_in(jax.random.fold_in(key, 6), position), (shards_of,), jnp.float32, low / len(pieces), high / len(pieces))
        gain = gain * jnp.repeat(jnp.exp(steps), dims[position] // shards_of).reshape((-1,) + (1,) * (len(dims) - 1 - position))
    return gain


def gaussian(rng, shape, scale, most, split=(), dtype=jnp.bfloat16):
    values = jax.random.normal(rng, shape, jnp.float32) * scale
    if len(split) > 0:
        values = shard_levels(rng, shape, split, -0.22, 0.18) * values
    return jnp.clip(values, min=-most, max=most).astype(dtype)


def setup_inputs(seed: int = 0, part: int = 0) -> dict:
    splits = jax.random.split(jax.random.key(seed), 5)
    part_splits = jax.random.split(jax.random.fold_in(splits[4], part), 5)
    return {
        "left_features": gaussian(part_splits[0], (H, W, C), 1.0, 6.0, ((0, 4), (1, 4))),
        "right_features": gaussian(part_splits[1], (H, W, C), 1.0, 6.0, ((0, 4), (1, 4))),
        "conv_first": gaussian(splits[2], (3, 3, DISP, DISP), (9 * DISP) ** -0.5, 0.125),
        "conv_second": gaussian(splits[3], (3, 3, DISP, DISP), (9 * DISP) ** -0.5, 0.125),
    }


def correlate(left_part, extended, disparities, chan_count):
    row_count, col_count = (left_part.shape[0], left_part.shape[1])
    block_count = col_count // disparities
    left_blocks = left_part.astype(jnp.float32).reshape(row_count, block_count, disparities, chan_count)
    right_blocks = extended.astype(jnp.float32).reshape(row_count, block_count + 1, disparities, chan_count)
    windows = jnp.concatenate((right_blocks[:, :-1], right_blocks[:, 1:]), axis=2)
    scores = jnp.einsum('rjwc,rjvc->rjwv', left_blocks, windows, precision=lax.Precision.HIGHEST)
    scores = scores * (1.0 / jnp.sqrt(jnp.float32(chan_count)))
    flat_scores = scores.reshape(row_count, block_count, disparities * 2 * disparities)
    flat_scores = jnp.pad(flat_scores, ((0, 0), (0, 0), (0, disparities)))
    skewed = flat_scores.reshape(row_count, block_count, disparities, 2 * disparities + 1)
    banded = skewed[..., 1:disparities + 1][..., ::-1]
    return banded.reshape(row_count, col_count, disparities).astype(jnp.bfloat16)

def convolve_same(image, kernel):
    result = lax.conv_general_dilated(image.astype(jnp.float32)[None], kernel.astype(jnp.float32), (1, 1), 'SAME', dimension_numbers=('NHWC', 'HWIO', 'NHWC'), precision=lax.Precision.HIGHEST)
    return result[0]

def reference(left_features, right_features, conv_first, conv_second):
    zero_cols = jnp.zeros((H, DISP, C), jnp.bfloat16)
    extended = jnp.concatenate((zero_cols, right_features), axis=1)

    def one_row(pair):
        return correlate(pair[0][None], pair[1][None], DISP, C)[0]
    volume = lax.map(one_row, (left_features, extended))
    hidden = jax.nn.relu(convolve_same(volume, conv_first)).astype(jnp.bfloat16)
    return jax.nn.relu(convolve_same(hidden, conv_second)).astype(jnp.bfloat16)
```

```python
import functools

import jax
import jax.numpy as jnp
from jax import lax
from jax.experimental import pallas as pl
from jax.experimental.pallas import tpu as pltpu
from jax.sharding import PartitionSpec as P

BF = jnp.bfloat16
F32 = jnp.float32
HALO = 16


class Segment:
    def __init__(self, base, outs):
        self.base, self.outs = base, outs
        self.hid = outs + 16
        self.vol = outs + 32


def reversal(size):
    i = lax.broadcasted_iota(jnp.int32, (size, size), 0)
    j = lax.broadcasted_iota(jnp.int32, (size, size), 1)
    return jnp.where(i + j == size - 1, 1.0, 0.0).astype(BF)


def part_kernel(segments, ext, disp, *refs):
    if ext:
        (flags, l_any, r_any, a_any, b_any, zl_any, zr_any, ca_any, cb_any, k1_any, k2_any, _, out_any,
         lbuf, rbuf, rrev, vf, vs, hf, hs, obuf, k1, k2, sems, ksems, osems) = refs
        pad = HALO
        lpad = disp + HALO
    else:
        (flags, l_any, r_any, a_any, b_any, k1_any, k2_any, out_any,
         lbuf, rbuf, rrev, vf, vs, hf, hs, obuf, k1, k2, sems, ksems, osems) = refs
        pad = 0
        lpad = 0
    rows, cols, chans = l_any.shape
    scale = 1.0 / (chans ** 0.5)
    odd = flags[0] == 1

    def copies(group):
        def own():
            lo, n = (0, rows // 2) if group == 1 else (rows // 2, rows - rows // 2)
            src, dst = pl.ds(lo, n), pl.ds(lo + 2, n)
            out = [
                (l_any.at[src], lbuf.at[dst, pl.ds(pad, cols)], sems.at[group]),
                (r_any.at[src], rbuf.at[dst, pl.ds(lpad, cols)], sems.at[group]),
            ]
            if ext:
                out += edges(zl_any.at[src], zr_any.at[src], dst)
            return out

        def edges(zl, zr, dst):
            return [
                (zl.at[:, pl.ds(0, lpad)], rbuf.at[dst, pl.ds(0, lpad)], sems.at[group]),
                (zl.at[:, pl.ds(lpad, pad)], lbuf.at[dst, pl.ds(0, pad)], sems.at[group]),
                (zr.at[:, pl.ds(0, pad)], rbuf.at[dst, pl.ds(lpad + cols, pad)], sems.at[group]),
                (zr.at[:, pl.ds(pad, pad)], lbuf.at[dst, pl.ds(pad + cols, pad)], sems.at[group]),
            ]

        def rim(main, corner):
            dst = pl.ds(0 if group == 0 else rows + 2, 2)
            out = [
                (main.at[:, pl.ds(0, cols)], lbuf.at[dst, pl.ds(pad, cols)], sems.at[group]),
                (main.at[:, pl.ds(cols, cols)], rbuf.at[dst, pl.ds(lpad, cols)], sems.at[group]),
            ]
            if ext:
                out += edges(corner.at[:, pl.ds(0, lpad + pad)], corner.at[:, pl.ds(lpad + pad, 2 * pad)], dst)
            return out

        if group in (1, 2):
            return own(), own()
        first = rim(a_any, ca_any if ext else None)
        second = rim(b_any, cb_any if ext else None)
        return (first, second) if group == 0 else (second, first)

    for group in range(4):
        if_odd, if_even = copies(group)
        if group in (1, 2):
            for c in if_odd:
                pltpu.make_async_copy(*c).start()
        else:
            @pl.when(odd)
            def _():
                for c in if_odd:
                    pltpu.make_async_copy(*c).start()

            @pl.when(jnp.logical_not(odd))
            def _():
                for c in if_even:
                    pltpu.make_async_copy(*c).start()
        if group == 0:
            k1_copy = pltpu.make_async_copy(k1_any, k1, ksems.at[0])
            k1_copy.start()
    k2_copy = pltpu.make_async_copy(k2_any, k2, ksems.at[1])
    k2_copy.start()

    def group_of(row):
        return 0 if row < 2 else 3 if row >= rows + 2 else 1 if row < 2 + rows // 2 else 2

    waited = set()

    def wait_rows(row):
        g = group_of(row)
        if g not in waited:
            waited.add(g)
            for c in copies(g)[0]:
                pltpu.make_async_copy(*c).wait()

    flip = reversal(128)

    def volume_rows(row):
        wait_rows(row)
        wait_rows(row + 1)
        dst_off = 0
        for s, seg in enumerate(segments):
            blocks = -(-seg.vol // 128)
            span = 128 * blocks + disp
            start = seg.base - disp + lpad
            have = seg.vol + disp
            for t in range(-(-have // 128)):
                n = min(128, have - 128 * t)
                both = jnp.concatenate([rbuf[row + q, start + 128 * t:start + 128 * t + n, :] for q in range(2)], axis=1)
                j = flip if n == 128 else reversal(n)
                res = jnp.dot(j, both, preferred_element_type=F32).astype(BF)
                for q in range(2):
                    rrev[s, row % 4 + q, span - 128 * t - n:span - 128 * t, :] = res[:, chans * q:chans * (q + 1)]
            for q in range(2):
                slot = row % 4 + q
                for b in range(blocks):
                    n = min(128, seg.vol - 128 * b)
                    u = 128 * (blocks - 1 - b)
                    left = lbuf[row + q, seg.base + pad + 128 * b:seg.base + pad + 128 * b + n, :]
                    scores = lax.dot_general(left, rrev[s, slot, u:u + 128 + disp, :], (((1,), (1,)), ((), ())),
                                             preferred_element_type=F32) * scale
                    rolled = pltpu.roll(scores, 1, 1, stride=1, stride_axis=0)
                    for h in range(disp // 128):
                        vf[slot, h, dst_off + 128 * b:dst_off + 128 * b + n, :] = rolled[:, 128 * (h + 1):128 * (h + 2)]
            dst_off += seg.vol
        for q in range(2):
            slot = row % 4 + q
            src, dst = 0, 0
            for seg in segments:
                for b in range(3):
                    for h in range(disp // 128):
                        vs[row + q, dst:dst + seg.hid, disp * b + 128 * h:disp * b + 128 * (h + 1)] = (
                            vf[slot, h, pl.ds(src + 14 + b, seg.hid), :].astype(BF))
                src += seg.vol
                dst += seg.hid

    def conv(src, row, kernel, count):
        m, k = src.shape[1], src.shape[2]
        x = jnp.concatenate([src[row + a:row + a + count].reshape(count * m, k) for a in range(3)], axis=1)
        return jnp.maximum(jnp.dot(x, kernel[...], preferred_element_type=F32), 0.0)

    m_hid = sum(seg.hid for seg in segments)
    m_out = sum(seg.outs for seg in segments)

    def hidden_rows(row, count):
        res = conv(vs, row, k1, count)
        for q in range(count):
            slot = (row + q) % 4
            one = res[q * m_hid:(q + 1) * m_hid]
            if row + q == 0:
                one = one * flags[1].astype(F32)
            if row + q == rows + 1:
                one = one * flags[2].astype(F32)
            for h in range(disp // 128):
                hf[slot, h] = one[:, 128 * h:128 * (h + 1)]
            src, dst = 0, 0
            for seg in segments:
                for edge, flag in ((-1, flags[3]), (cols, flags[4])):
                    pos = edge - (seg.base + 15)
                    if 0 <= pos < seg.outs + 2:
                        at = src + pos // 8 * 8
                        keep = lax.broadcasted_iota(jnp.int32, (8, 128), 0) != pos % 8
                        keep = jnp.where(keep, 1.0, flag.astype(F32))
                        for h in range(disp // 128):
                            hf[slot, h, at:at + 8, :] = hf[slot, h, at:at + 8, :] * keep
                for b in range(3):
                    for h in range(disp // 128):
                        hs[row + q, dst:dst + seg.outs, disp * b + 128 * h:disp * b + 128 * (h + 1)] = (
                            hf[slot, h, pl.ds(src + b, seg.outs), :].astype(BF))
                src += seg.hid
                dst += seg.outs

    pending = []

    def out_rows(row, count):
        res = conv(hs, row, k2, count).astype(BF)
        obuf[row:row + count] = res.reshape(count, m_out, disp)
        src = 0
        for s, seg in enumerate(segments):
            c = pltpu.make_async_copy(
                obuf.at[pl.ds(row, count), pl.ds(src, seg.outs)],
                out_any.at[pl.ds(row, count), pl.ds(seg.base + 16, seg.outs)], osems.at[row, s])
            c.start()
            pending.append(c)
            src += seg.outs

    volume_rows(0)
    volume_rows(2)
    k1_copy.wait()
    step = 2
    for row in range(0, rows + 2, step):
        if row + 4 < rows + 4:
            volume_rows(row + 4)
        hidden_rows(row, step)
        if row == 2:
            k2_copy.wait()
        if row >= 4:
            out_rows(row - 4, step)
    out_rows(rows - 2, step)
    for c in pending:
        c.wait()


def part_call(segments, ext, disp, rows, cols, chans, out_shape, operands):
    m_vol = sum(s.vol for s in segments)
    m_hid = sum(s.hid for s in segments)
    m_out = sum(s.outs for s in segments)
    pad = HALO if ext else 0
    span = max(128 * -(-s.vol // 128) + disp for s in segments)
    scratch = [
        pltpu.VMEM((rows + 4, cols + 2 * pad, chans), BF),
        pltpu.VMEM((rows + 4, cols + 2 * pad + (disp if ext else 0), chans), BF),
        pltpu.VMEM((len(segments), 4, span, chans), BF),
        pltpu.VMEM((4, disp // 128, m_vol, 128), F32),
        pltpu.VMEM((rows + 4, m_hid, 3 * disp), BF),
        pltpu.VMEM((4, disp // 128, m_hid, 128), F32),
        pltpu.VMEM((rows + 2, m_out, 3 * disp), BF),
        pltpu.VMEM((rows, m_out, disp), BF),
        pltpu.VMEM((9 * disp, disp), BF),
        pltpu.VMEM((9 * disp, disp), BF),
        pltpu.SemaphoreType.DMA((4,)),
        pltpu.SemaphoreType.DMA((2,)),
        pltpu.SemaphoreType.DMA((rows, len(segments))),
    ]
    flops = 2 * 9 * disp * disp * ((rows + 2) * m_hid + rows * m_out)
    return pl.pallas_call(
        functools.partial(part_kernel, segments, ext, disp),
        out_shape=out_shape,
        in_specs=[pl.BlockSpec(memory_space=pltpu.SMEM)] + [pl.BlockSpec(memory_space=pl.ANY)] * (len(operands) - 1),
        out_specs=pl.BlockSpec(memory_space=pl.ANY),
        scratch_shapes=scratch,
        input_output_aliases={len(operands) - 1: 0} if ext else {},
        compiler_params=pltpu.CompilerParams(vmem_limit_bytes=44 << 20),
        cost_estimate=pl.CostEstimate(flops=flops, bytes_accessed=6 << 20, transcendentals=0),
    )(*operands)


def pair_permute(x, axis, first):
    n = lax.axis_size(axis)
    perm = []
    for i in range(first, n - 1, 2):
        perm += [(i, i + 1), (i + 1, i)]
    return lax.ppermute(x, axis, perm)


def local(left, right, conv_first, conv_second):
    rows, cols, chans = left.shape
    disp = conv_first.shape[2]
    n_row, n_col = lax.axis_size("row"), lax.axis_size("col")
    ri, ci = lax.axis_index("row"), lax.axis_index("col")
    odd = ri % 2
    flags = jnp.stack([odd, (ri > 0).astype(jnp.int32), (ri < n_row - 1).astype(jnp.int32),
                       (ci > 0).astype(jnp.int32), (ci < n_col - 1).astype(jnp.int32)]).astype(jnp.int32)
    k1 = conv_first.reshape(9 * disp, disp)
    k2 = conv_second.reshape(9 * disp, disp)

    zl_msg = jnp.concatenate([right[:, cols - disp - HALO:], left[:, cols - HALO:]], axis=1)
    zl = lax.ppermute(zl_msg, "col", [(i, i + 1) for i in range(n_col - 1)])

    a_at = jnp.where(odd == 1, 0, rows - 2)
    b_at = jnp.where(odd == 1, rows - 2, 0)

    def facing(at, arrays):
        return jnp.concatenate([lax.dynamic_slice_in_dim(x, at, 2, 0) for x in arrays], axis=1)

    b = pair_permute(facing(b_at, (left, right)), "row", 1)
    a = pair_permute(facing(a_at, (left, right)), "row", 0)
    zr_msg = jnp.concatenate([right[:, :HALO], left[:, :HALO]], axis=1)
    zr = lax.ppermute(zr_msg, "col", [(i + 1, i) for i in range(n_col - 1)])

    out_shape = jax.ShapeDtypeStruct((rows, cols, disp), BF)
    mid = [Segment(disp, cols - disp - 2 * HALO)]
    out = part_call(mid, False, disp, rows, cols, chans, out_shape, (flags, left, right, a, b, k1, k2))

    cb = pair_permute(facing(b_at, (zl, zr)), "row", 1)
    ca = pair_permute(facing(a_at, (zl, zr)), "row", 0)
    rest = [Segment(-HALO, disp + HALO), Segment(cols - 2 * HALO, HALO)]
    return part_call(rest, True, disp, rows, cols, chans, out_shape,
                     (flags, left, right, a, b, zl, zr, ca, cb, k1, k2, out))


def solution(mesh):
    spec = P(("strip", "row"), "col", None)
    return jax.shard_map(local, mesh=mesh, in_specs=(spec, spec, P(), P()), out_specs=spec, check_vma=False)
```

```python
import functools

import jax
import jax.numpy as jnp
from jax import lax
from jax.experimental import pallas as pl
from jax.experimental.pallas import tpu as pltpu
from jax.sharding import PartitionSpec as P

BF = jnp.bfloat16
F32 = jnp.float32
HALO = 16
LAG = 0


class Segment:
    def __init__(self, base, outs):
        self.base, self.outs = base, outs
        self.hid = outs + 16
        self.vol = outs + 32


def part_kernel(segments, ext, disp, *refs):
    refs = list(refs)
    flags, l_own, r_own, a_any, b_any = refs[:5]
    zl, zr, ca_any, cb_any = refs[5:9] if ext else (None,) * 4
    k1_any, k2_any = refs[9:11] if ext else refs[5:7]
    out_any, lrim, rrim, rrev, vf, vs, hf, hs, obuf, k1, k2, sems, osems = refs[-13:]
    rows, cols, chans = l_own.shape
    pad = HALO if ext else 0
    lpad = disp + HALO if ext else 0
    scale = 1.0 / (chans ** 0.5)
    odd = flags[0] == 1
    if not ext:
        out_any, done = refs[7:9]
        done[0] = flags[5]
        done[1] = flags[6]

    def rim(side, main, corner):
        dst = pl.ds(2 * side, 2)
        out = [
            (main.at[:, pl.ds(0, cols)], lrim.at[dst, pl.ds(pad, cols)], sems.at[side]),
            (main.at[:, pl.ds(cols, cols)], rrim.at[dst, pl.ds(lpad, cols)], sems.at[side]),
        ]
        if ext:
            wide = lpad + pad
            out += [
                (corner.at[:, pl.ds(0, lpad)], rrim.at[dst, pl.ds(0, lpad)], sems.at[side]),
                (corner.at[:, pl.ds(lpad, pad)], lrim.at[dst, pl.ds(0, pad)], sems.at[side]),
                (corner.at[:, pl.ds(wide, pad)], rrim.at[dst, pl.ds(lpad + cols, pad)], sems.at[side]),
                (corner.at[:, pl.ds(wide + pad, pad)], lrim.at[dst, pl.ds(pad + cols, pad)], sems.at[side]),
            ]
        return out

    @pl.when(odd)
    def _():
        for c in rim(0, a_any, ca_any) + rim(1, b_any, cb_any):
            pltpu.make_async_copy(*c).start()

    @pl.when(jnp.logical_not(odd))
    def _():
        for c in rim(0, b_any, cb_any) + rim(1, a_any, ca_any):
            pltpu.make_async_copy(*c).start()

    k1_copy = pltpu.make_async_copy(k1_any, k1, sems.at[2])
    k2_copy = pltpu.make_async_copy(k2_any, k2, sems.at[3])
    k1_copy.start()
    k2_copy.start()
    waited = set()

    def wait_rows(row):
        side = 0 if row < 2 else 1 if row >= rows + 2 else None
        if side is not None and side not in waited:
            waited.add(side)
            for c in rim(side, a_any, ca_any):
                pltpu.make_async_copy(*c).wait()

    def pieces(row, lo, n, right):
        if row < 2 or row >= rows + 2:
            at = row if row < 2 else row - rows
            ref, off = (rrim, lpad) if right else (lrim, pad)
            return [ref[at, lo + off:lo + off + n, :]]
        row -= 2
        out = []
        if lo < 0:
            m = min(n, -lo)
            at = lo + lpad if right else lo + lpad + pad
            out.append(zl[row, at:at + m, :])
            lo, n = lo + m, n - m
        if n and lo < cols:
            m = min(n, cols - lo)
            out.append((r_own if right else l_own)[row, lo:lo + m, :])
            lo, n = lo + m, n - m
        if n:
            at = lo - cols + (0 if right else pad)
            out.append(zr[row, at:at + n, :])
        return out

    def columns(row, lo, n, right):
        parts = pieces(row, lo, n, right)
        return parts[0] if len(parts) == 1 else jnp.concatenate(parts, axis=0)

    mirror = 7 - lax.broadcasted_iota(jnp.int32, (8, 128), 0)

    def flip(row):
        def unit(s, seg, t):
            span = 128 * -(-seg.vol // 128) + disp
            start = seg.base - disp + 128 * t
            n = min(128, seg.vol + disp - 128 * t)
            both = jnp.concatenate([columns(row + q, start, n, True) for q in range(2)], axis=1)
            wide = both.astype(F32)
            res = jnp.concatenate([jnp.concatenate([
                jnp.take_along_axis(wide[n - 8 * (i + 1):n - 8 * i, chans * q:chans * (q + 1)], mirror, axis=0,
                                    mode="promise_in_bounds") for q in range(2)], axis=1)
                for i in range(n // 8)], axis=0).astype(BF)
            for q in range(2):
                rrev[s, row + q, span - 128 * t - n:span - 128 * t, :] = res[:, chans * q:chans * (q + 1)]

        if row < rows + 4:
            wait_rows(row)
            wait_rows(row + 1)
            for s, seg in enumerate(segments):
                for t in range(-(-(seg.vol + disp) // 128)):
                    unit(s, seg, t)

    def volume(row, scores_now):
        slot = row

        def score(s, seg, dst, b):
            n = min(128, seg.vol - 128 * b)
            u = 128 * (-(-seg.vol // 128) - 1 - b)
            left = columns(row, seg.base + 128 * b, n, False)
            scores = lax.dot_general(left, rrev[s, slot, u:u + 128 + disp, :], (((1,), (1,)), ((), ())),
                                     preferred_element_type=F32) * scale
            rolled = pltpu.roll(scores, 1, 1, stride=1, stride_axis=0)
            for h in range(disp // 128):
                vf[slot, h, dst + 128 * b:dst + 128 * b + n, :] = rolled[:, 128 * (h + 1):128 * (h + 2)]

        def spread(b):
            src, dst = 0, 0
            for seg in segments:
                for h in range(disp // 128):
                    vs[row, dst:dst + seg.hid, disp * b + 128 * h:disp * b + 128 * (h + 1)] = (
                        vf[slot, h, pl.ds(src + 14 + b, seg.hid), :].astype(BF))
                src += seg.vol
                dst += seg.hid

        dst = 0
        if scores_now:
            for s, seg in enumerate(segments):
                for b in range(-(-seg.vol // 128)):
                    score(s, seg, dst, b)
                dst += seg.vol
        else:
            for b in range(3):
                spread(b)

    def conv(src, row, count, kernel):
        x = jnp.concatenate([src[row + a:row + a + count].reshape(count * src.shape[1], src.shape[2])
                             for a in range(3)], axis=1)
        res = jnp.maximum(jnp.dot(x, kernel[...], preferred_element_type=F32), 0.0)
        return [res[q * src.shape[1]:(q + 1) * src.shape[1]] for q in range(count)]

    m_hid = sum(seg.hid for seg in segments)
    m_out = sum(seg.outs for seg in segments)

    def hidden(row, count):
        for q, one in enumerate(conv(vs, row, count, k1)):
            if row + q == 0:
                one = one * flags[1].astype(F32)
            if row + q == rows + 1:
                one = one * flags[2].astype(F32)
            for h in range(disp // 128):
                hf[row + q, h] = one[:, 128 * h:128 * (h + 1)]

    def hidden_spreads(row):
        slot = row

        def spread(b):
            src, dst = 0, 0
            for seg in segments:
                for edge, flag in ((-1, flags[3]), (cols, flags[4])):
                    pos = edge - (seg.base + 15)
                    if b == 0 and 0 <= pos < seg.outs + 2:
                        at = src + pos // 8 * 8
                        keep = lax.broadcasted_iota(jnp.int32, (8, 128), 0) != pos % 8
                        keep = jnp.where(keep, 1.0, flag.astype(F32))
                        for h in range(disp // 128):
                            hf[slot, h, at:at + 8, :] = hf[slot, h, at:at + 8, :] * keep
                for h in range(disp // 128):
                    hs[row, dst:dst + seg.outs, disp * b + 128 * h:disp * b + 128 * (h + 1)] = (
                        hf[slot, h, pl.ds(src + b, seg.outs), :].astype(BF))
                src += seg.hid
                dst += seg.outs

        for b in range(3):
            spread(b)

    pending = []

    def out(row, count):
        for q, one in enumerate(conv(hs, row, count, k2)):
            obuf[row + q] = one.astype(BF)
        src = 0
        for s, seg in enumerate(segments):
            c = pltpu.make_async_copy(
                obuf.at[pl.ds(row, count), pl.ds(src, seg.outs)],
                out_any.at[pl.ds(row, count), pl.ds(seg.base + 16, seg.outs)], osems.at[row, s])
            c.start()
            pending.append(c)
            src += seg.outs

    def both(row, end, f, *args):
        if 0 <= row < end:
            f(row, *args)
            f(row + 1, *args)

    flip(2)
    flip(4)
    both(2, rows + 4, volume, True)
    flip(0)
    both(0, rows + 4, volume, True)
    both(2, rows + 4, volume, False)
    both(0, rows + 4, volume, False)
    k1_copy.wait()
    for row in range(0, rows + 6, 2):
        if row == 6:
            k2_copy.wait()
        both(row + 4, rows + 4, volume, True)
        if row < rows + 2:
            hidden(row, 2)
        if 6 <= row < rows + 6:
            out(row - 6, 2)
        flip(row + 6)
        both(row + 4, rows + 4, volume, False)
        both(row - 2 + LAG, rows + 2, hidden_spreads)
    for c in pending:
        c.wait()


def part_call(segments, ext, disp, rows, cols, chans, out_shape, operands):
    m_vol = sum(s.vol for s in segments)
    m_hid = sum(s.hid for s in segments)
    m_out = sum(s.outs for s in segments)
    pad = HALO if ext else 0
    span = max(128 * -(-s.vol // 128) + disp for s in segments)
    scratch = [
        pltpu.VMEM((4, cols + 2 * pad, chans), BF),
        pltpu.VMEM((4, cols + 2 * pad + (disp if ext else 0), chans), BF),
        pltpu.VMEM((len(segments), rows + 4, span, chans), BF),
        pltpu.VMEM((rows + 4, disp // 128, m_vol, 128), F32),
        pltpu.VMEM((rows + 4, m_hid, 3 * disp), BF),
        pltpu.VMEM((rows + 2, disp // 128, m_hid, 128), F32),
        pltpu.VMEM((rows + 2, m_out, 3 * disp), BF),
        pltpu.VMEM((rows, m_out, disp), BF),
        pltpu.VMEM((9 * disp, disp), BF),
        pltpu.VMEM((9 * disp, disp), BF),
        pltpu.SemaphoreType.DMA((4,)),
        pltpu.SemaphoreType.DMA((rows, len(segments))),
    ]
    vmem, anywhere = pl.BlockSpec(memory_space=pltpu.VMEM), pl.BlockSpec(memory_space=pltpu.HBM)
    smem = pl.BlockSpec(memory_space=pltpu.SMEM)
    flops = 2 * 9 * disp * disp * ((rows + 2) * m_hid + rows * m_out)
    return pl.pallas_call(
        functools.partial(part_kernel, segments, ext, disp),
        out_shape=out_shape if ext else [out_shape, jax.ShapeDtypeStruct((2,), jnp.int32)],
        in_specs=([smem, vmem, vmem, anywhere, anywhere] + ([vmem, vmem, anywhere, anywhere] if ext else [])
                  + [anywhere, anywhere] + ([anywhere] if ext else [])),
        out_specs=anywhere if ext else [anywhere, smem],
        scratch_shapes=scratch,
        input_output_aliases={len(operands) - 1: 0} if ext else {},
        compiler_params=pltpu.CompilerParams(vmem_limit_bytes=54 << 20),
        cost_estimate=pl.CostEstimate(flops=flops if ext else 1 << 20, bytes_accessed=1 << 20, transcendentals=0),
    )(*operands)


def pair_permute(x, axis, first):
    n = lax.axis_size(axis)
    perm = []
    for i in range(first, n - 1, 2):
        perm += [(i, i + 1), (i + 1, i)]
    return lax.ppermute(x, axis, perm)


def copy_all(copies, sems):
    copies = [pltpu.make_async_copy(src, dst, sems.at[i]) for i, (src, dst) in enumerate(copies)]
    for c in copies:
        c.start()
    for c in copies:
        c.wait()


def pack_columns(l_any, r_any, zl, sems):
    rows, cols, _ = l_any.shape
    wide = zl.shape[1] - HALO
    copies = [(r_any.at[q, pl.ds(cols - wide, wide)], zl.at[q, pl.ds(0, wide)]) for q in range(rows)]
    copies.append((l_any.at[:, pl.ds(cols - HALO, HALO)], zl.at[:, pl.ds(wide, HALO)]))
    copy_all(copies, sems)


def pack_rims(flags, l_any, r_any, a, b, zr, sems):
    cols = l_any.shape[1]
    copies = []
    for msg, at in ((b, flags[6]), (a, flags[5])):
        copies.append((l_any.at[pl.ds(at, 2)], msg.at[:, pl.ds(0, cols)]))
        copies.append((r_any.at[pl.ds(at, 2)], msg.at[:, pl.ds(cols, cols)]))
    copies.append((r_any.at[:, pl.ds(0, HALO)], zr.at[:, pl.ds(0, HALO)]))
    copies.append((l_any.at[:, pl.ds(0, HALO)], zr.at[:, pl.ds(HALO, HALO)]))
    copy_all(copies, sems)


def pack(flags, left, right, disp):
    rows, cols, chans = left.shape
    anywhere = pl.BlockSpec(memory_space=pl.ANY)
    zl = pl.pallas_call(
        pack_columns,
        out_shape=jax.ShapeDtypeStruct((rows, disp + 2 * HALO, chans), BF),
        in_specs=[pl.BlockSpec(memory_space=pltpu.HBM)] * 2,
        out_specs=anywhere,
        scratch_shapes=[pltpu.SemaphoreType.DMA((rows + 1,))],
        compiler_params=pltpu.CompilerParams(vmem_limit_bytes=1 << 20),
        cost_estimate=pl.CostEstimate(flops=0, bytes_accessed=1 << 20, transcendentals=0),
    )(left, right)
    shapes = [(2, 2 * cols, chans), (2, 2 * cols, chans), (rows, 2 * HALO, chans)]
    return [zl] + list(pl.pallas_call(
        pack_rims,
        out_shape=[jax.ShapeDtypeStruct(s, BF) for s in shapes],
        in_specs=[pl.BlockSpec(memory_space=pltpu.SMEM)] + [pl.BlockSpec(memory_space=pltpu.HBM)] * 2,
        out_specs=[anywhere] * 3,
        scratch_shapes=[pltpu.SemaphoreType.DMA((6,))],
        compiler_params=pltpu.CompilerParams(vmem_limit_bytes=1 << 20),
        cost_estimate=pl.CostEstimate(flops=20 << 30, bytes_accessed=1 << 20, transcendentals=0),
    )(flags, left, right))


def local(left, right, conv_first, conv_second):
    rows, cols, chans = left.shape
    disp = conv_first.shape[2]
    n_row, n_col = lax.axis_size("row"), lax.axis_size("col")
    ri, ci = lax.axis_index("row"), lax.axis_index("col")
    odd = ri % 2
    a_at = jnp.where(odd == 1, 0, rows - 2)
    b_at = jnp.where(odd == 1, rows - 2, 0)
    flags = jnp.stack([odd, ri > 0, ri < n_row - 1, ci > 0, ci < n_col - 1, a_at, b_at]).astype(jnp.int32)
    k1 = conv_first.reshape(9 * disp, disp)
    k2 = conv_second.reshape(9 * disp, disp)

    zl_msg, a_msg, b_msg, zr_msg = pack(flags, left, right, disp)
    zl = lax.ppermute(zl_msg, "col", [(i, i + 1) for i in range(n_col - 1)])
    b = pair_permute(b_msg, "row", 1)
    a = pair_permute(a_msg, "row", 0)
    zr = lax.ppermute(zr_msg, "col", [(i + 1, i) for i in range(n_col - 1)])

    out_shape = jax.ShapeDtypeStruct((rows, cols, disp), BF)
    mid = [Segment(disp, cols - disp - 2 * HALO)]
    out, done = part_call(mid, False, disp, rows, cols, chans, out_shape, (flags, left, right, a, b, k1, k2))

    def facing(at):
        return jnp.concatenate([lax.dynamic_slice_in_dim(x, at, 2, 0) for x in (zl, zr)], axis=1)

    cb = pair_permute(facing(done[1]), "row", 1)
    ca = pair_permute(facing(done[0]), "row", 0)
    rest = [Segment(-HALO, disp + HALO), Segment(cols - 2 * HALO, HALO)]
    return part_call(rest, True, disp, rows, cols, chans, out_shape,
                     (flags, left, right, a, b, zl, zr, ca, cb, k1, k2, out))


def solution(mesh):
    spec = P(("strip", "row"), "col", None)
    return jax.shard_map(local, mesh=mesh, in_specs=(spec, spec, P(), P()), out_specs=spec, check_vma=False)
```

```python
import functools

import jax
import jax.numpy as jnp
from jax import lax
from jax.experimental import pallas as pl
from jax.experimental.pallas import tpu as pltpu
from jax.sharding import PartitionSpec as P

BF = jnp.bfloat16
F32 = jnp.float32
HALO = 16
PACK = 60


class Segment:
    def __init__(self, base, outs):
        self.base, self.outs = base, outs
        self.hid = outs + 16
        self.vol = outs + 32


def part_kernel(segments, ext, disp, *refs):
    refs = list(refs)
    flags, l_own, r_own, a_any, b_any = refs[:5]
    zl, zr, ca_any, cb_any = refs[5:9] if ext else (None,) * 4
    k1, k2 = refs[9:11] if ext else refs[5:7]
    out_any, lrim, rrim, rrev, vf, vs, hf, hs, obuf, sems, osems = refs[-11:]
    rows, cols, chans = l_own.shape
    pad = HALO if ext else 0
    lpad = disp + HALO if ext else 0
    scale = 1.0 / (chans ** 0.5)
    odd = flags[0] == 1
    if not ext:
        out_any = refs[7]

    def rim(side, main, corner):
        dst = pl.ds(2 * side, 2)
        out = [
            (main.at[:, pl.ds(0, cols)], lrim.at[dst, pl.ds(pad, cols)], sems.at[side]),
            (main.at[:, pl.ds(cols, cols)], rrim.at[dst, pl.ds(lpad, cols)], sems.at[side]),
        ]
        if ext:
            wide = lpad + pad
            out += [
                (corner.at[:, pl.ds(0, lpad)], rrim.at[dst, pl.ds(0, lpad)], sems.at[side]),
                (corner.at[:, pl.ds(lpad, pad)], lrim.at[dst, pl.ds(0, pad)], sems.at[side]),
                (corner.at[:, pl.ds(wide, pad)], rrim.at[dst, pl.ds(lpad + cols, pad)], sems.at[side]),
                (corner.at[:, pl.ds(wide + pad, pad)], lrim.at[dst, pl.ds(pad + cols, pad)], sems.at[side]),
            ]
        return out

    @pl.when(odd)
    def _():
        for c in rim(0, a_any, ca_any) + rim(1, b_any, cb_any):
            pltpu.make_async_copy(*c).start()

    @pl.when(jnp.logical_not(odd))
    def _():
        for c in rim(0, b_any, cb_any) + rim(1, a_any, ca_any):
            pltpu.make_async_copy(*c).start()

    waited = set()

    def wait_rows(row):
        side = 0 if row < 2 else 1 if row >= rows + 2 else None
        if side is not None and side not in waited:
            waited.add(side)
            for c in rim(side, a_any, ca_any):
                pltpu.make_async_copy(*c).wait()

    def pieces(row, lo, n, right):
        if row < 2 or row >= rows + 2:
            at = row if row < 2 else row - rows
            ref, off = (rrim, lpad) if right else (lrim, pad)
            return [ref[at, lo + off:lo + off + n, :]]
        row -= 2
        out = []
        if lo < 0:
            m = min(n, -lo)
            at = lo + lpad if right else lo + lpad + pad
            out.append(zl[row, at:at + m, :])
            lo, n = lo + m, n - m
        if n and lo < cols:
            m = min(n, cols - lo)
            out.append((r_own if right else l_own)[row, lo:lo + m, :])
            lo, n = lo + m, n - m
        if n:
            at = lo - cols + (0 if right else pad)
            out.append(zr[row, at:at + n, :])
        return out

    def columns(row, lo, n, right):
        parts = pieces(row, lo, n, right)
        return parts[0] if len(parts) == 1 else jnp.concatenate(parts, axis=0)

    mirror = 7 - lax.broadcasted_iota(jnp.int32, (8, 128), 0)

    def flip(row):
        def unit(s, seg, t):
            span = 128 * -(-seg.vol // 128) + disp
            start = seg.base - disp + 128 * t
            n = min(128, seg.vol + disp - 128 * t)
            both = jnp.concatenate([columns(row + q, start, n, True) for q in range(2)], axis=1)
            wide = both.astype(F32)
            res = jnp.concatenate([jnp.concatenate([
                jnp.take_along_axis(wide[n - 8 * (i + 1):n - 8 * i, chans * q:chans * (q + 1)], mirror, axis=0,
                                    mode="promise_in_bounds") for q in range(2)], axis=1)
                for i in range(n // 8)], axis=0).astype(BF)
            for q in range(2):
                rrev[s, row + q, span - 128 * t - n:span - 128 * t, :] = res[:, chans * q:chans * (q + 1)]

        if row < rows + 4:
            wait_rows(row)
            wait_rows(row + 1)
            for s, seg in enumerate(segments):
                for t in range(-(-(seg.vol + disp) // 128)):
                    unit(s, seg, t)

    def volume(row, scores_now):
        slot = row

        def score(s, seg, dst, b):
            n = min(128, seg.vol - 128 * b)
            u = 128 * (-(-seg.vol // 128) - 1 - b)
            left = columns(row, seg.base + 128 * b, n, False)
            scores = lax.dot_general(left, rrev[s, slot, u:u + 128 + disp, :], (((1,), (1,)), ((), ())),
                                     preferred_element_type=F32) * scale
            rolled = pltpu.roll(scores, 1, 1, stride=1, stride_axis=0)
            for h in range(disp // 128):
                vf[slot, h, dst + 128 * b:dst + 128 * b + n, :] = rolled[:, 128 * (h + 1):128 * (h + 2)]

        def spread(b):
            src, dst = 0, 0
            for seg in segments:
                for h in range(disp // 128):
                    vs[row, dst:dst + seg.hid, disp * b + 128 * h:disp * b + 128 * (h + 1)] = (
                        vf[slot, h, pl.ds(src + 14 + b, seg.hid), :].astype(BF))
                src += seg.vol
                dst += seg.hid

        dst = 0
        if scores_now:
            for s, seg in enumerate(segments):
                for b in range(-(-seg.vol // 128)):
                    score(s, seg, dst, b)
                dst += seg.vol
        else:
            for b in range(3):
                spread(b)

    def conv(src, row, count, kernel):
        x = jnp.concatenate([src[row + a:row + a + count].reshape(count * src.shape[1], src.shape[2])
                             for a in range(3)], axis=1)
        res = jnp.maximum(jnp.dot(x, kernel[...], preferred_element_type=F32), 0.0)
        return [res[q * src.shape[1]:(q + 1) * src.shape[1]] for q in range(count)]

    m_hid = sum(seg.hid for seg in segments)
    m_out = sum(seg.outs for seg in segments)

    def hidden(row, count):
        for q, one in enumerate(conv(vs, row, count, k1)):
            if row + q == 0:
                one = one * flags[1].astype(F32)
            if row + q == rows + 1:
                one = one * flags[2].astype(F32)
            for h in range(disp // 128):
                hf[row + q, h] = one[:, 128 * h:128 * (h + 1)]

    def hidden_spreads(row):
        slot = row

        def spread(b):
            src, dst = 0, 0
            for seg in segments:
                for edge, flag in ((-1, flags[3]), (cols, flags[4])):
                    pos = edge - (seg.base + 15)
                    if b == 0 and 0 <= pos < seg.outs + 2:
                        at = src + pos // 8 * 8
                        keep = lax.broadcasted_iota(jnp.int32, (8, 128), 0) != pos % 8
                        keep = jnp.where(keep, 1.0, flag.astype(F32))
                        for h in range(disp // 128):
                            hf[slot, h, at:at + 8, :] = hf[slot, h, at:at + 8, :] * keep
                for h in range(disp // 128):
                    hs[row, dst:dst + seg.outs, disp * b + 128 * h:disp * b + 128 * (h + 1)] = (
                        hf[slot, h, pl.ds(src + b, seg.outs), :].astype(BF))
                src += seg.hid
                dst += seg.outs

        for b in range(3):
            spread(b)

    pending = []

    def out(row, count):
        for q, one in enumerate(conv(hs, row, count, k2)):
            obuf[row + q] = one.astype(BF)
        src = 0
        for s, seg in enumerate(segments):
            c = pltpu.make_async_copy(
                obuf.at[pl.ds(row, count), pl.ds(src, seg.outs)],
                out_any.at[pl.ds(row, count), pl.ds(seg.base + 16, seg.outs)], osems.at[row, s])
            c.start()
            pending.append(c)
            src += seg.outs

    def both(row, end, f, *args):
        if 0 <= row < end:
            f(row, *args)
            f(row + 1, *args)

    flip(2)
    flip(4)
    both(2, rows + 4, volume, True)
    flip(0)
    both(0, rows + 4, volume, True)
    both(2, rows + 4, volume, False)
    both(0, rows + 4, volume, False)
    for row in range(0, rows + 6, 2):
        both(row + 4, rows + 4, volume, True)
        if row < rows + 2:
            hidden(row, 2)
        if 6 <= row < rows + 6:
            out(row - 6, 2)
        flip(row + 6)
        both(row + 4, rows + 4, volume, False)
        both(row - 2, rows + 2, hidden_spreads)
    for c in pending:
        c.wait()


def part_call(segments, ext, disp, rows, cols, chans, out_shape, operands):
    m_vol = sum(s.vol for s in segments)
    m_hid = sum(s.hid for s in segments)
    m_out = sum(s.outs for s in segments)
    pad = HALO if ext else 0
    span = max(128 * -(-s.vol // 128) + disp for s in segments)
    scratch = [
        pltpu.VMEM((4, cols + 2 * pad, chans), BF),
        pltpu.VMEM((4, cols + 2 * pad + (disp if ext else 0), chans), BF),
        pltpu.VMEM((len(segments), rows + 4, span, chans), BF),
        pltpu.VMEM((rows + 4, disp // 128, m_vol, 128), F32),
        pltpu.VMEM((rows + 4, m_hid, 3 * disp), BF),
        pltpu.VMEM((rows + 2, disp // 128, m_hid, 128), F32),
        pltpu.VMEM((rows + 2, m_out, 3 * disp), BF),
        pltpu.VMEM((rows, m_out, disp), BF),
        pltpu.SemaphoreType.DMA((2,)),
        pltpu.SemaphoreType.DMA((rows, len(segments))),
    ]
    vmem, anywhere = pl.BlockSpec(memory_space=pltpu.VMEM), pl.BlockSpec(memory_space=pl.ANY)
    smem = pl.BlockSpec(memory_space=pltpu.SMEM)
    flops = 2 * 9 * disp * disp * ((rows + 2) * m_hid + rows * m_out)
    return pl.pallas_call(
        functools.partial(part_kernel, segments, ext, disp),
        out_shape=out_shape if ext else [out_shape, jax.ShapeDtypeStruct((16, 128), BF)],
        in_specs=([smem, vmem, vmem, anywhere, anywhere] + ([vmem, vmem, anywhere, anywhere] if ext else [])
                  + [vmem, vmem] + ([anywhere] if ext else [])),
        out_specs=anywhere if ext else [anywhere, anywhere],
        scratch_shapes=scratch,
        input_output_aliases={len(operands) - 1: 0} if ext else {},
        compiler_params=pltpu.CompilerParams(vmem_limit_bytes=44 << 20),
        cost_estimate=pl.CostEstimate(flops=flops, bytes_accessed=6 << 20, transcendentals=0),
    )(*operands)


def pair_permute(x, axis, first):
    n = lax.axis_size(axis)
    perm = []
    for i in range(first, n - 1, 2):
        perm += [(i, i + 1), (i + 1, i)]
    return lax.ppermute(x, axis, perm)


def copy_all(copies, sems):
    copies = [pltpu.make_async_copy(src, dst, sems.at[i]) for i, (src, dst) in enumerate(copies)]
    for c in copies:
        c.start()
    for c in copies:
        c.wait()


def pack_columns(l_any, r_any, zl, sems):
    rows, cols, _ = l_any.shape
    wide = zl.shape[1] - HALO
    copies = [(r_any.at[q, pl.ds(cols - wide, wide)], zl.at[q, pl.ds(0, wide)]) for q in range(rows)]
    copies.append((l_any.at[:, pl.ds(cols - HALO, HALO)], zl.at[:, pl.ds(wide, HALO)]))
    copy_all(copies, sems)


def pack_rims(flags, l_any, r_any, a, b, zr, sems):
    cols = l_any.shape[1]
    copies = []
    for msg, at in ((b, flags[6]), (a, flags[5])):
        copies.append((l_any.at[pl.ds(at, 2)], msg.at[:, pl.ds(0, cols)]))
        copies.append((r_any.at[pl.ds(at, 2)], msg.at[:, pl.ds(cols, cols)]))
    copies.append((r_any.at[:, pl.ds(0, HALO)], zr.at[:, pl.ds(0, HALO)]))
    copies.append((l_any.at[:, pl.ds(0, HALO)], zr.at[:, pl.ds(HALO, HALO)]))
    copy_all(copies, sems)


def pack(flags, left, right, disp):
    rows, cols, chans = left.shape
    anywhere = pl.BlockSpec(memory_space=pl.ANY)
    zl = pl.pallas_call(
        pack_columns,
        out_shape=jax.ShapeDtypeStruct((rows, disp + 2 * HALO, chans), BF),
        in_specs=[pl.BlockSpec(memory_space=pl.ANY)] * 2,
        out_specs=anywhere,
        scratch_shapes=[pltpu.SemaphoreType.DMA((rows + 1,))],
        compiler_params=pltpu.CompilerParams(vmem_limit_bytes=PACK << 20),
        cost_estimate=pl.CostEstimate(flops=0, bytes_accessed=1 << 10, transcendentals=0),
    )(left, right)
    shapes = [(2, 2 * cols, chans), (2, 2 * cols, chans), (rows, 2 * HALO, chans)]
    return [zl] + list(pl.pallas_call(
        pack_rims,
        out_shape=[jax.ShapeDtypeStruct(s, BF) for s in shapes],
        in_specs=[pl.BlockSpec(memory_space=pltpu.SMEM)] + [pl.BlockSpec(memory_space=pl.ANY)] * 2,
        out_specs=[anywhere] * 3,
        scratch_shapes=[pltpu.SemaphoreType.DMA((6,))],
        compiler_params=pltpu.CompilerParams(vmem_limit_bytes=PACK << 20),
        cost_estimate=pl.CostEstimate(flops=0, bytes_accessed=1 << 10, transcendentals=0),
    )(flags, left, right))


def pack_corners_kernel(flags, zl, zr, _, ca, cb, sems):
    wide = zl.shape[1]
    copies = []
    for msg, at in ((cb, flags[6]), (ca, flags[5])):
        copies.append((zl.at[pl.ds(at, 2)], msg.at[:, pl.ds(0, wide)]))
        copies.append((zr.at[pl.ds(at, 2)], msg.at[:, pl.ds(wide, 2 * HALO)]))
    copy_all(copies, sems)


def pack_corners(flags, zl, zr, after):
    anywhere = pl.BlockSpec(memory_space=pl.ANY)
    shape = jax.ShapeDtypeStruct((2, zl.shape[1] + zr.shape[1], zl.shape[2]), BF)
    return pl.pallas_call(
        pack_corners_kernel,
        out_shape=[shape, shape],
        in_specs=[pl.BlockSpec(memory_space=pltpu.SMEM)] + [anywhere] * 3,
        out_specs=[anywhere] * 2,
        scratch_shapes=[pltpu.SemaphoreType.DMA((4,))],
        compiler_params=pltpu.CompilerParams(vmem_limit_bytes=1 << 20),
        cost_estimate=pl.CostEstimate(flops=0, bytes_accessed=1 << 10, transcendentals=0),
    )(flags, zl, zr, after)


def local(left, right, conv_first, conv_second):
    rows, cols, chans = left.shape
    disp = conv_first.shape[2]
    n_row, n_col = lax.axis_size("row"), lax.axis_size("col")
    ri, ci = lax.axis_index("row"), lax.axis_index("col")
    odd = ri % 2
    a_at = jnp.where(odd == 1, 0, rows - 2)
    b_at = jnp.where(odd == 1, rows - 2, 0)
    flags = jnp.stack([odd, ri > 0, ri < n_row - 1, ci > 0, ci < n_col - 1, a_at, b_at]).astype(jnp.int32)
    k1 = conv_first.reshape(9 * disp, disp)
    k2 = conv_second.reshape(9 * disp, disp)

    zl_msg, a_msg, b_msg, zr_msg = pack(flags, left, right, disp)
    zl = lax.ppermute(zl_msg, "col", [(i, i + 1) for i in range(n_col - 1)])
    b = pair_permute(b_msg, "row", 1)
    a = pair_permute(a_msg, "row", 0)
    zr = lax.ppermute(zr_msg, "col", [(i + 1, i) for i in range(n_col - 1)])

    out_shape = jax.ShapeDtypeStruct((rows, cols, disp), BF)
    mid = [Segment(disp, cols - disp - 2 * HALO)]
    out, after = part_call(mid, False, disp, rows, cols, chans, out_shape, (flags, left, right, a, b, k1, k2))

    ca_msg, cb_msg = pack_corners(flags, zl, zr, after)
    cb = pair_permute(cb_msg, "row", 1)
    ca = pair_permute(ca_msg, "row", 0)
    rest = [Segment(-HALO, disp + HALO), Segment(cols - 2 * HALO, HALO)]
    return part_call(rest, True, disp, rows, cols, chans, out_shape,
                     (flags, left, right, a, b, zl, zr, ca, cb, k1, k2, out))


def solution(mesh):
    spec = P(("strip", "row"), "col", None)
    return jax.shard_map(local, mesh=mesh, in_specs=(spec, spec, P(), P()), out_specs=spec, check_vma=False)
```

```python
import functools

import jax
import jax.numpy as jnp
from jax import lax
from jax.experimental import pallas as pl
from jax.experimental.pallas import tpu as pltpu
from jax.sharding import PartitionSpec as P

BF = jnp.bfloat16
F32 = jnp.float32
HALO = 16
PACK = 60


class Segment:
    def __init__(self, base, outs):
        self.base, self.outs = base, outs
        self.hid = outs + 16
        self.vol = outs + 32


def part_kernel(segments, ext, disp, *refs):
    refs = list(refs)
    flags, l_own, r_own, a_ref, b_ref = refs[:5]
    zl, zr, ca, cb = refs[5:9] if ext else (None,) * 4
    k1, k2 = refs[9:11] if ext else refs[5:7]
    out_any, (rrev, vf, vs, hf, hs, obuf, osems) = refs[-9 if not ext else -8], refs[-7:]
    rows, cols, chans = l_own.shape
    pad = HALO if ext else 0
    lpad = disp + HALO if ext else 0
    scale = 1.0 / (chans ** 0.5)
    odd = flags[0].astype(F32)

    def pieces(row, lo, n, right, own, left_edge, right_edge):
        out = []
        if lo < 0:
            m = min(n, -lo)
            at = left_edge[1] + lo + lpad if right else left_edge[1] + lpad + pad + lo
            out.append(left_edge[0][row, at:at + m, :])
            lo, n = lo + m, n - m
        if n and lo < cols:
            m = min(n, cols - lo)
            out.append(own[0][row, own[1] + lo:own[1] + lo + m, :])
            lo, n = lo + m, n - m
        if n:
            at = right_edge[1] + lo - cols + (0 if right else pad)
            out.append(right_edge[0][row, at:at + n, :])
        return out[0] if len(out) == 1 else jnp.concatenate(out, axis=0)

    def columns(row, lo, n, right):
        if 2 <= row < rows + 2:
            return pieces(row - 2, lo, n, right, (r_own if right else l_own, 0), (zl, 0), (zr, 0))
        at, share = (row, odd) if row < 2 else (row - rows - 2, 1.0 - odd)
        start = cols if right else 0
        one = pieces(at, lo, n, right, (a_ref, start), (ca, 0), (ca, lpad + pad))
        two = pieces(at, lo, n, right, (b_ref, start), (cb, 0), (cb, lpad + pad))
        return (one.astype(F32) * share + two.astype(F32) * (1.0 - share)).astype(BF)

    mirror = 7 - lax.broadcasted_iota(jnp.int32, (8, 128), 0)

    def flip(row):
        def unit(s, seg, t):
            span = 128 * -(-seg.vol // 128) + disp
            start = seg.base - disp + 128 * t
            n = min(128, seg.vol + disp - 128 * t)
            both = jnp.concatenate([columns(row + q, start, n, True) for q in range(2)], axis=1)
            wide = both.astype(F32)
            res = jnp.concatenate([jnp.concatenate([
                jnp.take_along_axis(wide[n - 8 * (i + 1):n - 8 * i, chans * q:chans * (q + 1)], mirror, axis=0,
                                    mode="promise_in_bounds") for q in range(2)], axis=1)
                for i in range(n // 8)], axis=0).astype(BF)
            for q in range(2):
                rrev[s, row + q, span - 128 * t - n:span - 128 * t, :] = res[:, chans * q:chans * (q + 1)]

        if row < rows + 4:
            for s, seg in enumerate(segments):
                for t in range(-(-(seg.vol + disp) // 128)):
                    unit(s, seg, t)

    def volume(row, scores_now):
        slot = row

        def score(s, seg, dst, b):
            n = min(128, seg.vol - 128 * b)
            u = 128 * (-(-seg.vol // 128) - 1 - b)
            left = columns(row, seg.base + 128 * b, n, False)
            scores = lax.dot_general(left, rrev[s, slot, u:u + 128 + disp, :], (((1,), (1,)), ((), ())),
                                     preferred_element_type=F32) * scale
            rolled = pltpu.roll(scores, 1, 1, stride=1, stride_axis=0)
            for h in range(disp // 128):
                vf[slot, h, dst + 128 * b:dst + 128 * b + n, :] = rolled[:, 128 * (h + 1):128 * (h + 2)]

        def spread(b):
            src, dst = 0, 0
            for seg in segments:
                for h in range(disp // 128):
                    vs[row, dst:dst + seg.hid, disp * b + 128 * h:disp * b + 128 * (h + 1)] = (
                        vf[slot, h, pl.ds(src + 14 + b, seg.hid), :].astype(BF))
                src += seg.vol
                dst += seg.hid

        dst = 0
        if scores_now:
            for s, seg in enumerate(segments):
                for b in range(-(-seg.vol // 128)):
                    score(s, seg, dst, b)
                dst += seg.vol
        else:
            for b in range(3):
                spread(b)

    def conv(src, row, count, kernel):
        x = jnp.concatenate([src[row + a:row + a + count].reshape(count * src.shape[1], src.shape[2])
                             for a in range(3)], axis=1)
        res = jnp.maximum(jnp.dot(x, kernel[...], preferred_element_type=F32), 0.0)
        return [res[q * src.shape[1]:(q + 1) * src.shape[1]] for q in range(count)]

    m_hid = sum(seg.hid for seg in segments)
    m_out = sum(seg.outs for seg in segments)

    def hidden(row, count):
        for q, one in enumerate(conv(vs, row, count, k1)):
            if row + q == 0:
                one = one * flags[1].astype(F32)
            if row + q == rows + 1:
                one = one * flags[2].astype(F32)
            for h in range(disp // 128):
                hf[row + q, h] = one[:, 128 * h:128 * (h + 1)]

    def hidden_spreads(row):
        slot = row

        def spread(b):
            src, dst = 0, 0
            for seg in segments:
                for edge, flag in ((-1, flags[3]), (cols, flags[4])):
                    pos = edge - (seg.base + 15)
                    if b == 0 and 0 <= pos < seg.outs + 2:
                        at = src + pos // 8 * 8
                        keep = lax.broadcasted_iota(jnp.int32, (8, 128), 0) != pos % 8
                        keep = jnp.where(keep, 1.0, flag.astype(F32))
                        for h in range(disp // 128):
                            hf[slot, h, at:at + 8, :] = hf[slot, h, at:at + 8, :] * keep
                for h in range(disp // 128):
                    hs[row, dst:dst + seg.outs, disp * b + 128 * h:disp * b + 128 * (h + 1)] = (
                        hf[slot, h, pl.ds(src + b, seg.outs), :].astype(BF))
                src += seg.hid
                dst += seg.outs

        for b in range(3):
            spread(b)

    pending = []

    def out(row, count):
        for q, one in enumerate(conv(hs, row, count, k2)):
            obuf[row + q] = one.astype(BF)
        src = 0
        for s, seg in enumerate(segments):
            c = pltpu.make_async_copy(
                obuf.at[pl.ds(row, count), pl.ds(src, seg.outs)],
                out_any.at[pl.ds(row, count), pl.ds(seg.base + 16, seg.outs)], osems.at[row, s])
            c.start()
            pending.append(c)
            src += seg.outs

    def both(row, end, f, *args):
        if 0 <= row < end:
            f(row, *args)
            f(row + 1, *args)

    flip(2)
    flip(4)
    both(2, rows + 4, volume, True)
    flip(0)
    both(0, rows + 4, volume, True)
    both(2, rows + 4, volume, False)
    both(0, rows + 4, volume, False)
    for row in range(0, rows + 6, 2):
        both(row + 4, rows + 4, volume, True)
        if row < rows + 2:
            hidden(row, 2)
        if 6 <= row < rows + 6:
            out(row - 6, 2)
        flip(row + 6)
        both(row + 4, rows + 4, volume, False)
        both(row - 2, rows + 2, hidden_spreads)
    for c in pending:
        c.wait()


def part_call(segments, ext, disp, rows, cols, chans, out_shape, operands):
    m_vol = sum(s.vol for s in segments)
    m_hid = sum(s.hid for s in segments)
    m_out = sum(s.outs for s in segments)
    pad = HALO if ext else 0
    span = max(128 * -(-s.vol // 128) + disp for s in segments)
    scratch = [
        pltpu.VMEM((len(segments), rows + 4, span, chans), BF),
        pltpu.VMEM((rows + 4, disp // 128, m_vol, 128), F32),
        pltpu.VMEM((rows + 4, m_hid, 3 * disp), BF),
        pltpu.VMEM((rows + 2, disp // 128, m_hid, 128), F32),
        pltpu.VMEM((rows + 2, m_out, 3 * disp), BF),
        pltpu.VMEM((rows, m_out, disp), BF),
        pltpu.SemaphoreType.DMA((rows, len(segments))),
    ]
    vmem, anywhere = pl.BlockSpec(memory_space=pltpu.VMEM), pl.BlockSpec(memory_space=pl.ANY)
    smem = pl.BlockSpec(memory_space=pltpu.SMEM)
    flops = 2 * 9 * disp * disp * ((rows + 2) * m_hid + rows * m_out)
    return pl.pallas_call(
        functools.partial(part_kernel, segments, ext, disp),
        out_shape=out_shape if ext else [out_shape, jax.ShapeDtypeStruct((16, 128), BF)],
        in_specs=([smem] + [vmem] * (8 if ext else 4)
                  + [vmem, vmem] + ([anywhere] if ext else [])),
        out_specs=anywhere if ext else [anywhere, anywhere],
        scratch_shapes=scratch,
        input_output_aliases={len(operands) - 1: 0} if ext else {},
        compiler_params=pltpu.CompilerParams(vmem_limit_bytes=44 << 20),
        cost_estimate=pl.CostEstimate(flops=flops, bytes_accessed=6 << 20, transcendentals=0),
    )(*operands)


def pair_permute(x, axis, first):
    n = lax.axis_size(axis)
    perm = []
    for i in range(first, n - 1, 2):
        perm += [(i, i + 1), (i + 1, i)]
    return lax.ppermute(x, axis, perm)


def copy_all(copies, sems):
    copies = [pltpu.make_async_copy(src, dst, sems.at[i]) for i, (src, dst) in enumerate(copies)]
    for c in copies:
        c.start()
    for c in copies:
        c.wait()


def pack_kernel(flags, l_any, r_any, zl, a, b, zr, zl_buf, a_buf, b_buf, zr_buf, in_sems, out_sems):
    rows, cols, _ = l_any.shape
    wide = zl.shape[1] - HALO
    half = rows // 2
    fills = {
        0: [(r_any.at[pl.ds(0, half), pl.ds(cols - wide, wide)], zl_buf.at[pl.ds(0, half), pl.ds(0, wide)]),
                 (r_any.at[pl.ds(half, rows - half), pl.ds(cols - wide, wide)],
                  zl_buf.at[pl.ds(half, rows - half), pl.ds(0, wide)]),
                 (l_any.at[:, pl.ds(cols - HALO, HALO)], zl_buf.at[:, pl.ds(wide, HALO)])],
        3: [(r_any.at[:, pl.ds(0, HALO)], zr_buf.at[:, pl.ds(0, HALO)]),
                 (l_any.at[:, pl.ds(0, HALO)], zr_buf.at[:, pl.ds(HALO, HALO)])],
    }
    for i, buf, at in ((1, b_buf, flags[6]), (2, a_buf, flags[5])):
        fills[i] = [(l_any.at[pl.ds(at, 2)], buf.at[:, pl.ds(0, cols)]),
                      (r_any.at[pl.ds(at, 2)], buf.at[:, pl.ds(cols, cols)])]
    order = ((zl_buf, zl), (b_buf, b), (a_buf, a), (zr_buf, zr))
    started = []
    for i, (buf, _) in enumerate(order):
        started.append([pltpu.make_async_copy(src, dst, in_sems.at[i, j]) for j, (src, dst) in enumerate(fills[i])])
        for c in started[-1]:
            c.start()
    sends = []
    for i, (buf, msg) in enumerate(order):
        for c in started[i]:
            c.wait()
        sends.append(pltpu.make_async_copy(buf, msg, out_sems.at[i]))
        sends[-1].start()
    for c in sends:
        c.wait()


def pack(flags, left, right, disp):
    rows, cols, chans = left.shape
    anywhere = pl.BlockSpec(memory_space=pl.ANY)
    shapes = [(rows, disp + 2 * HALO, chans), (2, 2 * cols, chans), (2, 2 * cols, chans), (rows, 2 * HALO, chans)]
    return pl.pallas_call(
        pack_kernel,
        out_shape=[jax.ShapeDtypeStruct(s, BF) for s in shapes],
        in_specs=[pl.BlockSpec(memory_space=pltpu.SMEM), anywhere, anywhere],
        out_specs=[anywhere] * 4,
        scratch_shapes=[pltpu.VMEM(s, BF) for s in shapes]
        + [pltpu.SemaphoreType.DMA((4, 3)), pltpu.SemaphoreType.DMA((4,))],
        compiler_params=pltpu.CompilerParams(vmem_limit_bytes=PACK << 20),
        cost_estimate=pl.CostEstimate(flops=0, bytes_accessed=1 << 10, transcendentals=0),
    )(flags, left, right)


def pack_corners_kernel(flags, zl, zr, _, ca, cb, sems):
    wide = zl.shape[1]
    copies = []
    for msg, at in ((cb, flags[6]), (ca, flags[5])):
        copies.append((zl.at[pl.ds(at, 2)], msg.at[:, pl.ds(0, wide)]))
        copies.append((zr.at[pl.ds(at, 2)], msg.at[:, pl.ds(wide, 2 * HALO)]))
    copy_all(copies, sems)


def pack_corners(flags, zl, zr, after):
    anywhere = pl.BlockSpec(memory_space=pl.ANY)
    shape = jax.ShapeDtypeStruct((2, zl.shape[1] + zr.shape[1], zl.shape[2]), BF)
    return pl.pallas_call(
        pack_corners_kernel,
        out_shape=[shape, shape],
        in_specs=[pl.BlockSpec(memory_space=pltpu.SMEM)] + [anywhere] * 3,
        out_specs=[anywhere] * 2,
        scratch_shapes=[pltpu.SemaphoreType.DMA((4,))],
        compiler_params=pltpu.CompilerParams(vmem_limit_bytes=1 << 20),
        cost_estimate=pl.CostEstimate(flops=0, bytes_accessed=1 << 10, transcendentals=0),
    )(flags, zl, zr, after)


def local(left, right, conv_first, conv_second):
    rows, cols, chans = left.shape
    disp = conv_first.shape[2]
    n_row, n_col = lax.axis_size("row"), lax.axis_size("col")
    ri, ci = lax.axis_index("row"), lax.axis_index("col")
    odd = ri % 2
    a_at = jnp.where(odd == 1, 0, rows - 2)
    b_at = jnp.where(odd == 1, rows - 2, 0)
    flags = jnp.stack([odd, ri > 0, ri < n_row - 1, ci > 0, ci < n_col - 1, a_at, b_at]).astype(jnp.int32)
    k1 = conv_first.reshape(9 * disp, disp)
    k2 = conv_second.reshape(9 * disp, disp)

    zl_msg, a_msg, b_msg, zr_msg = pack(flags, left, right, disp)
    zl = lax.ppermute(zl_msg, "col", [(i, i + 1) for i in range(n_col - 1)])
    b = pair_permute(b_msg, "row", 1)
    a = pair_permute(a_msg, "row", 0)
    zr = lax.ppermute(zr_msg, "col", [(i + 1, i) for i in range(n_col - 1)])

    out_shape = jax.ShapeDtypeStruct((rows, cols, disp), BF)
    mid = [Segment(disp, cols - disp - 2 * HALO)]
    out, after = part_call(mid, False, disp, rows, cols, chans, out_shape, (flags, left, right, a, b, k1, k2))

    ca_msg, cb_msg = pack_corners(flags, zl, zr, after)
    cb = pair_permute(cb_msg, "row", 1)
    ca = pair_permute(ca_msg, "row", 0)
    rest = [Segment(-HALO, disp + HALO), Segment(cols - 2 * HALO, HALO)]
    return part_call(rest, True, disp, rows, cols, chans, out_shape,
                     (flags, left, right, a, b, zl, zr, ca, cb, k1, k2, out))


def solution(mesh):
    spec = P(("strip", "row"), "col", None)
    return jax.shard_map(local, mesh=mesh, in_specs=(spec, spec, P(), P()), out_specs=spec, check_vma=False)
```

```python
import functools

import jax
import jax.numpy as jnp
from jax import lax
from jax.experimental import pallas as pl
from jax.experimental.pallas import tpu as pltpu
from jax.sharding import PartitionSpec as P

BF = jnp.bfloat16
F32 = jnp.float32
HALO = 16
PACK = 58


class Segment:
    def __init__(self, base, outs):
        self.base, self.outs = base, outs
        self.hid = outs + 16
        self.vol = outs + 32


def part_kernel(segments, ext, disp, *refs):
    refs = list(refs)
    flags, l_own, r_own, a_ref, b_ref = refs[:5]
    zl, zr, ca, cb = refs[5:9] if ext else (None,) * 4
    k1, k2 = refs[9:11] if ext else refs[5:7]
    out_any, (rrev, vf, vs, hf, hs, obuf, osems) = refs[-9 if not ext else -8], refs[-7:]
    rows, cols, chans = l_own.shape
    pad = HALO if ext else 0
    lpad = disp + HALO if ext else 0
    scale = 1.0 / (chans ** 0.5)
    odd = flags[0].astype(F32)

    def pieces(row, lo, n, right, own, left_edge, right_edge):
        out = []
        if lo < 0:
            m = min(n, -lo)
            at = left_edge[1] + lo + lpad if right else left_edge[1] + lpad + pad + lo
            out.append(left_edge[0][row, at:at + m, :])
            lo, n = lo + m, n - m
        if n and lo < cols:
            m = min(n, cols - lo)
            out.append(own[0][row, own[1] + lo:own[1] + lo + m, :])
            lo, n = lo + m, n - m
        if n:
            at = right_edge[1] + lo - cols + (0 if right else pad)
            out.append(right_edge[0][row, at:at + n, :])
        return out[0] if len(out) == 1 else jnp.concatenate(out, axis=0)

    def columns(row, lo, n, right):
        if 2 <= row < rows + 2:
            return pieces(row - 2, lo, n, right, (r_own if right else l_own, 0), (zl, 0), (zr, 0))
        at, share = (row, odd) if row < 2 else (row - rows - 2, 1.0 - odd)
        start = cols if right else 0
        one = pieces(at, lo, n, right, (a_ref, start), (ca, 0), (ca, lpad + pad))
        two = pieces(at, lo, n, right, (b_ref, start), (cb, 0), (cb, lpad + pad))
        return (one.astype(F32) * share + two.astype(F32) * (1.0 - share)).astype(BF)

    mirror = 7 - lax.broadcasted_iota(jnp.int32, (8, 128), 0)

    def flip(row):
        def unit(s, seg, t):
            span = 128 * -(-seg.vol // 128) + disp
            start = seg.base - disp + 128 * t
            n = min(128, seg.vol + disp - 128 * t)
            both = jnp.concatenate([columns(row + q, start, n, True) for q in range(2)], axis=1)
            wide = both.astype(F32)
            res = jnp.concatenate([jnp.concatenate([
                jnp.take_along_axis(wide[n - 8 * (i + 1):n - 8 * i, chans * q:chans * (q + 1)], mirror, axis=0,
                                    mode="promise_in_bounds") for q in range(2)], axis=1)
                for i in range(n // 8)], axis=0).astype(BF)
            for q in range(2):
                rrev[s, row + q, span - 128 * t - n:span - 128 * t, :] = res[:, chans * q:chans * (q + 1)]

        if row < rows + 4:
            for s, seg in enumerate(segments):
                for t in range(-(-(seg.vol + disp) // 128)):
                    unit(s, seg, t)

    def volume(row, scores_now):
        slot = row

        def score(s, seg, dst, b):
            n = min(128, seg.vol - 128 * b)
            u = 128 * (-(-seg.vol // 128) - 1 - b)
            left = columns(row, seg.base + 128 * b, n, False)
            scores = lax.dot_general(left, rrev[s, slot, u:u + 128 + disp, :], (((1,), (1,)), ((), ())),
                                     preferred_element_type=F32) * scale
            rolled = pltpu.roll(scores, 1, 1, stride=1, stride_axis=0)
            for h in range(disp // 128):
                vf[slot, h, dst + 128 * b:dst + 128 * b + n, :] = rolled[:, 128 * (h + 1):128 * (h + 2)]

        def spread(b):
            src, dst = 0, 0
            for seg in segments:
                for h in range(disp // 128):
                    vs[row, dst:dst + seg.hid, disp * b + 128 * h:disp * b + 128 * (h + 1)] = (
                        vf[slot, h, pl.ds(src + 14 + b, seg.hid), :].astype(BF))
                src += seg.vol
                dst += seg.hid

        dst = 0
        if scores_now:
            for s, seg in enumerate(segments):
                for b in range(-(-seg.vol // 128)):
                    score(s, seg, dst, b)
                dst += seg.vol
        else:
            for b in range(3):
                spread(b)

    def conv(src, row, count, kernel):
        x = jnp.concatenate([src[row + a:row + a + count].reshape(count * src.shape[1], src.shape[2])
                             for a in range(3)], axis=1)
        res = jnp.maximum(jnp.dot(x, kernel[...], preferred_element_type=F32), 0.0)
        return [res[q * src.shape[1]:(q + 1) * src.shape[1]] for q in range(count)]

    m_hid = sum(seg.hid for seg in segments)
    m_out = sum(seg.outs for seg in segments)

    def hidden(row, count):
        for q, one in enumerate(conv(vs, row, count, k1)):
            if row + q == 0:
                one = one * flags[1].astype(F32)
            if row + q == rows + 1:
                one = one * flags[2].astype(F32)
            for h in range(disp // 128):
                hf[row + q, h] = one[:, 128 * h:128 * (h + 1)]

    def hidden_spreads(row):
        slot = row

        def spread(b):
            src, dst = 0, 0
            for seg in segments:
                for edge, flag in ((-1, flags[3]), (cols, flags[4])):
                    pos = edge - (seg.base + 15)
                    if b == 0 and 0 <= pos < seg.outs + 2:
                        at = src + pos // 8 * 8
                        keep = lax.broadcasted_iota(jnp.int32, (8, 128), 0) != pos % 8
                        keep = jnp.where(keep, 1.0, flag.astype(F32))
                        for h in range(disp // 128):
                            hf[slot, h, at:at + 8, :] = hf[slot, h, at:at + 8, :] * keep
                for h in range(disp // 128):
                    hs[row, dst:dst + seg.outs, disp * b + 128 * h:disp * b + 128 * (h + 1)] = (
                        hf[slot, h, pl.ds(src + b, seg.outs), :].astype(BF))
                src += seg.hid
                dst += seg.outs

        for b in range(3):
            spread(b)

    pending = []

    def out(row, count):
        for q, one in enumerate(conv(hs, row, count, k2)):
            obuf[row + q] = one.astype(BF)
        src = 0
        for s, seg in enumerate(segments):
            c = pltpu.make_async_copy(
                obuf.at[pl.ds(row, count), pl.ds(src, seg.outs)],
                out_any.at[pl.ds(row, count), pl.ds(seg.base + 16, seg.outs)], osems.at[row, s])
            c.start()
            pending.append(c)
            src += seg.outs

    def both(row, end, f, *args):
        if 0 <= row < end:
            f(row, *args)
            f(row + 1, *args)

    flip(2)
    flip(4)
    both(2, rows + 4, volume, True)
    flip(0)
    both(0, rows + 4, volume, True)
    both(2, rows + 4, volume, False)
    both(0, rows + 4, volume, False)
    for row in range(0, rows + 6, 2):
        both(row + 4, rows + 4, volume, True)
        if row < rows + 2:
            hidden(row, 2)
        if 6 <= row < rows + 6:
            out(row - 6, 2)
        flip(row + 6)
        both(row + 4, rows + 4, volume, False)
        both(row - 2, rows + 2, hidden_spreads)
    for c in pending:
        c.wait()


def part_call(segments, ext, disp, rows, cols, chans, out_shape, operands):
    m_vol = sum(s.vol for s in segments)
    m_hid = sum(s.hid for s in segments)
    m_out = sum(s.outs for s in segments)
    pad = HALO if ext else 0
    span = max(128 * -(-s.vol // 128) + disp for s in segments)
    scratch = [
        pltpu.VMEM((len(segments), rows + 4, span, chans), BF),
        pltpu.VMEM((rows + 4, disp // 128, m_vol, 128), F32),
        pltpu.VMEM((rows + 4, m_hid, 3 * disp), BF),
        pltpu.VMEM((rows + 2, disp // 128, m_hid, 128), F32),
        pltpu.VMEM((rows + 2, m_out, 3 * disp), BF),
        pltpu.VMEM((rows, m_out, disp), BF),
        pltpu.SemaphoreType.DMA((rows, len(segments))),
    ]
    vmem, anywhere = pl.BlockSpec(memory_space=pltpu.VMEM), pl.BlockSpec(memory_space=pl.ANY)
    smem = pl.BlockSpec(memory_space=pltpu.SMEM)
    flops = 2 * 9 * disp * disp * ((rows + 2) * m_hid + rows * m_out)
    return pl.pallas_call(
        functools.partial(part_kernel, segments, ext, disp),
        out_shape=out_shape if ext else [out_shape, jax.ShapeDtypeStruct((16, 128), BF)],
        in_specs=([smem] + [vmem] * (8 if ext else 4)
                  + [vmem, vmem] + ([anywhere] if ext else [])),
        out_specs=anywhere if ext else [anywhere, anywhere],
        scratch_shapes=scratch,
        input_output_aliases={len(operands) - 1: 0} if ext else {},
        compiler_params=pltpu.CompilerParams(vmem_limit_bytes=44 << 20),
        cost_estimate=pl.CostEstimate(flops=flops, bytes_accessed=6 << 20, transcendentals=0),
    )(*operands)


def pair_permute(x, axis, first):
    n = lax.axis_size(axis)
    perm = []
    for i in range(first, n - 1, 2):
        perm += [(i, i + 1), (i + 1, i)]
    return lax.ppermute(x, axis, perm)


def copy_all(copies, sems):
    copies = [pltpu.make_async_copy(src, dst, sems.at[i]) for i, (src, dst) in enumerate(copies)]
    for c in copies:
        c.start()
    for c in copies:
        c.wait()


def pack_kernel(flags, l_any, r_any, zl, a, b, zr, zl_buf, a_buf, b_buf, zr_buf, in_sems, out_sems):
    rows, cols, _ = l_any.shape
    wide = zl.shape[1] - HALO
    half = rows // 2
    fills = {
        0: [(r_any.at[pl.ds(0, half), pl.ds(cols - wide, wide)], zl_buf.at[pl.ds(0, half), pl.ds(0, wide)]),
                 (r_any.at[pl.ds(half, rows - half), pl.ds(cols - wide, wide)],
                  zl_buf.at[pl.ds(half, rows - half), pl.ds(0, wide)]),
                 (l_any.at[:, pl.ds(cols - HALO, HALO)], zl_buf.at[:, pl.ds(wide, HALO)])],
        3: [(r_any.at[:, pl.ds(0, HALO)], zr_buf.at[:, pl.ds(0, HALO)]),
                 (l_any.at[:, pl.ds(0, HALO)], zr_buf.at[:, pl.ds(HALO, HALO)])],
    }
    for i, buf, at in ((1, b_buf, flags[6]), (2, a_buf, flags[5])):
        fills[i] = [(l_any.at[pl.ds(at, 2)], buf.at[:, pl.ds(0, cols)]),
                      (r_any.at[pl.ds(at, 2)], buf.at[:, pl.ds(cols, cols)])]
    order = ((zl_buf, zl), (b_buf, b), (a_buf, a), (zr_buf, zr))
    started = []
    for i, (buf, _) in enumerate(order):
        started.append([pltpu.make_async_copy(src, dst, in_sems.at[i, j]) for j, (src, dst) in enumerate(fills[i])])
        for c in started[-1]:
            c.start()
    sends = []
    for i, (buf, msg) in enumerate(order):
        for c in started[i]:
            c.wait()
        sends.append(pltpu.make_async_copy(buf, msg, out_sems.at[i]))
        sends[-1].start()
    for c in sends:
        c.wait()


def pack(flags, left, right, disp):
    rows, cols, chans = left.shape
    anywhere = pl.BlockSpec(memory_space=pl.ANY)
    shapes = [(rows, disp + 2 * HALO, chans), (2, 2 * cols, chans), (2, 2 * cols, chans), (rows, 2 * HALO, chans)]
    return pl.pallas_call(
        pack_kernel,
        out_shape=[jax.ShapeDtypeStruct(s, BF) for s in shapes],
        in_specs=[pl.BlockSpec(memory_space=pltpu.SMEM), anywhere, anywhere],
        out_specs=[anywhere] * 4,
        scratch_shapes=[pltpu.VMEM(s, BF) for s in shapes]
        + [pltpu.SemaphoreType.DMA((4, 3)), pltpu.SemaphoreType.DMA((4,))],
        compiler_params=pltpu.CompilerParams(vmem_limit_bytes=PACK << 20),
        cost_estimate=pl.CostEstimate(flops=8 << 30, bytes_accessed=1 << 10, transcendentals=0),
    )(flags, left, right)


def pack_corners_kernel(flags, zl, zr, _, ca, cb, sems):
    wide = zl.shape[1]
    copies = []
    for msg, at in ((cb, flags[6]), (ca, flags[5])):
        copies.append((zl.at[pl.ds(at, 2)], msg.at[:, pl.ds(0, wide)]))
        copies.append((zr.at[pl.ds(at, 2)], msg.at[:, pl.ds(wide, 2 * HALO)]))
    copy_all(copies, sems)


def pack_corners(flags, zl, zr, after):
    anywhere = pl.BlockSpec(memory_space=pl.ANY)
    shape = jax.ShapeDtypeStruct((2, zl.shape[1] + zr.shape[1], zl.shape[2]), BF)
    return pl.pallas_call(
        pack_corners_kernel,
        out_shape=[shape, shape],
        in_specs=[pl.BlockSpec(memory_space=pltpu.SMEM)] + [anywhere] * 3,
        out_specs=[anywhere] * 2,
        scratch_shapes=[pltpu.SemaphoreType.DMA((4,))],
        compiler_params=pltpu.CompilerParams(vmem_limit_bytes=1 << 20),
        cost_estimate=pl.CostEstimate(flops=8 << 30, bytes_accessed=1 << 10, transcendentals=0),
    )(flags, zl, zr, after)


def local(left, right, conv_first, conv_second):
    rows, cols, chans = left.shape
    disp = conv_first.shape[2]
    n_row, n_col = lax.axis_size("row"), lax.axis_size("col")
    ri, ci = lax.axis_index("row"), lax.axis_index("col")
    odd = ri % 2
    a_at = jnp.where(odd == 1, 0, rows - 2)
    b_at = jnp.where(odd == 1, rows - 2, 0)
    flags = jnp.stack([odd, ri > 0, ri < n_row - 1, ci > 0, ci < n_col - 1, a_at, b_at]).astype(jnp.int32)
    k1 = conv_first.reshape(9 * disp, disp)
    k2 = conv_second.reshape(9 * disp, disp)

    zl_msg, a_msg, b_msg, zr_msg = pack(flags, left, right, disp)
    zl = lax.ppermute(zl_msg, "col", [(i, i + 1) for i in range(n_col - 1)])
    b = pair_permute(b_msg, "row", 1)
    a = pair_permute(a_msg, "row", 0)
    zr = lax.ppermute(zr_msg, "col", [(i + 1, i) for i in range(n_col - 1)])

    out_shape = jax.ShapeDtypeStruct((rows, cols, disp), BF)
    mid = [Segment(disp, cols - disp - 2 * HALO)]
    out, after = part_call(mid, False, disp, rows, cols, chans, out_shape, (flags, left, right, a, b, k1, k2))

    ca_msg, cb_msg = pack_corners(flags, zl, zr, after)
    cb = pair_permute(cb_msg, "row", 1)
    ca = pair_permute(ca_msg, "row", 0)
    rest = [Segment(-HALO, disp + HALO), Segment(cols - 2 * HALO, HALO)]
    return part_call(rest, True, disp, rows, cols, chans, out_shape,
                     (flags, left, right, a, b, zl, zr, ca, cb, k1, k2, out))


def solution(mesh):
    spec = P(("strip", "row"), "col", None)
    return jax.shard_map(local, mesh=mesh, in_specs=(spec, spec, P(), P()), out_specs=spec, check_vma=False)
```

```python
import functools

import jax
import jax.numpy as jnp
from jax import lax
from jax.experimental import pallas as pl
from jax.experimental.pallas import tpu as pltpu
from jax.sharding import PartitionSpec as P

BF = jnp.bfloat16
F32 = jnp.float32
HALO = 16
PACK = 58


class Segment:
    def __init__(self, base, outs):
        self.base, self.outs = base, outs
        self.hid = outs + 16
        self.vol = outs + 32


def part_kernel(segments, ext, disp, *refs):
    refs = list(refs)
    flags, l_own, r_own, a_ref, b_ref = refs[:5]
    zl, zr, ca, cb = refs[5:9] if ext else (None,) * 4
    k1, k2 = refs[9:11] if ext else refs[5:7]
    out_any, (rrev, vf, vs, hf, hs, obuf, osems) = refs[-8], refs[-7:]
    rows, cols, chans = l_own.shape
    pad = HALO if ext else 0
    lpad = disp + HALO if ext else 0
    scale = 1.0 / (chans ** 0.5)
    odd = flags[0].astype(F32)

    def pieces(row, lo, n, right, own, left_edge, right_edge):
        out = []
        if lo < 0:
            m = min(n, -lo)
            at = left_edge[1] + lo + lpad if right else left_edge[1] + lpad + pad + lo
            out.append(left_edge[0][row, at:at + m, :])
            lo, n = lo + m, n - m
        if n and lo < cols:
            m = min(n, cols - lo)
            out.append(own[0][row, own[1] + lo:own[1] + lo + m, :])
            lo, n = lo + m, n - m
        if n:
            at = right_edge[1] + lo - cols + (0 if right else pad)
            out.append(right_edge[0][row, at:at + n, :])
        return out[0] if len(out) == 1 else jnp.concatenate(out, axis=0)

    def columns(row, lo, n, right):
        if 2 <= row < rows + 2:
            return pieces(row - 2, lo, n, right, (r_own if right else l_own, 0), (zl, 0), (zr, 0))
        at, share = (row, odd) if row < 2 else (row - rows - 2, 1.0 - odd)
        start = cols if right else 0
        one = pieces(at, lo, n, right, (a_ref, start), (ca, 0), (ca, lpad + pad))
        two = pieces(at, lo, n, right, (b_ref, start), (cb, 0), (cb, lpad + pad))
        return (one.astype(F32) * share + two.astype(F32) * (1.0 - share)).astype(BF)

    mirror = 7 - lax.broadcasted_iota(jnp.int32, (8, 128), 0)

    def flip(row):
        def unit(s, seg, t):
            span = 128 * -(-seg.vol // 128) + disp
            start = seg.base - disp + 128 * t
            n = min(128, seg.vol + disp - 128 * t)
            both = jnp.concatenate([columns(row + q, start, n, True) for q in range(2)], axis=1)
            wide = both.astype(F32)
            res = jnp.concatenate([jnp.concatenate([
                jnp.take_along_axis(wide[n - 8 * (i + 1):n - 8 * i, chans * q:chans * (q + 1)], mirror, axis=0,
                                    mode="promise_in_bounds") for q in range(2)], axis=1)
                for i in range(n // 8)], axis=0).astype(BF)
            for q in range(2):
                rrev[s, row + q, span - 128 * t - n:span - 128 * t, :] = res[:, chans * q:chans * (q + 1)]

        if row < rows + 4:
            for s, seg in enumerate(segments):
                for t in range(-(-(seg.vol + disp) // 128)):
                    unit(s, seg, t)

    def volume(row, scores_now):
        slot = row

        def score(s, seg, dst, b):
            n = min(128, seg.vol - 128 * b)
            u = 128 * (-(-seg.vol // 128) - 1 - b)
            left = columns(row, seg.base + 128 * b, n, False)
            scores = lax.dot_general(left, rrev[s, slot, u:u + 128 + disp, :], (((1,), (1,)), ((), ())),
                                     preferred_element_type=F32) * scale
            rolled = pltpu.roll(scores, 1, 1, stride=1, stride_axis=0)
            for h in range(disp // 128):
                vf[slot, h, dst + 128 * b:dst + 128 * b + n, :] = rolled[:, 128 * (h + 1):128 * (h + 2)]

        def spread(b):
            src, dst = 0, 0
            for seg in segments:
                for h in range(disp // 128):
                    vs[row, dst:dst + seg.hid, disp * b + 128 * h:disp * b + 128 * (h + 1)] = (
                        vf[slot, h, pl.ds(src + 14 + b, seg.hid), :].astype(BF))
                src += seg.vol
                dst += seg.hid

        dst = 0
        if scores_now:
            for s, seg in enumerate(segments):
                for b in range(-(-seg.vol // 128)):
                    score(s, seg, dst, b)
                dst += seg.vol
        else:
            for b in range(3):
                spread(b)

    def conv(src, row, count, kernel):
        x = jnp.concatenate([src[row + a:row + a + count].reshape(count * src.shape[1], src.shape[2])
                             for a in range(3)], axis=1)
        res = jnp.maximum(jnp.dot(x, kernel[...], preferred_element_type=F32), 0.0)
        return [res[q * src.shape[1]:(q + 1) * src.shape[1]] for q in range(count)]

    m_hid = sum(seg.hid for seg in segments)
    m_out = sum(seg.outs for seg in segments)

    def hidden(row, count):
        for q, one in enumerate(conv(vs, row, count, k1)):
            if row + q == 0:
                one = one * flags[1].astype(F32)
            if row + q == rows + 1:
                one = one * flags[2].astype(F32)
            for h in range(disp // 128):
                hf[row + q, h] = one[:, 128 * h:128 * (h + 1)]

    def hidden_spreads(row):
        slot = row

        def spread(b):
            src, dst = 0, 0
            for seg in segments:
                for edge, flag in ((-1, flags[3]), (cols, flags[4])):
                    pos = edge - (seg.base + 15)
                    if b == 0 and 0 <= pos < seg.outs + 2:
                        at = src + pos // 8 * 8
                        keep = lax.broadcasted_iota(jnp.int32, (8, 128), 0) != pos % 8
                        keep = jnp.where(keep, 1.0, flag.astype(F32))
                        for h in range(disp // 128):
                            hf[slot, h, at:at + 8, :] = hf[slot, h, at:at + 8, :] * keep
                for h in range(disp // 128):
                    hs[row, dst:dst + seg.outs, disp * b + 128 * h:disp * b + 128 * (h + 1)] = (
                        hf[slot, h, pl.ds(src + b, seg.outs), :].astype(BF))
                src += seg.hid
                dst += seg.outs

        for b in range(3):
            spread(b)

    pending = []

    def out(row, count):
        for q, one in enumerate(conv(hs, row, count, k2)):
            obuf[row + q] = one.astype(BF)
        src = 0
        for s, seg in enumerate(segments):
            c = pltpu.make_async_copy(
                obuf.at[pl.ds(row, count), pl.ds(src, seg.outs)],
                out_any.at[pl.ds(row, count), pl.ds(seg.base + 16, seg.outs)], osems.at[row, s])
            c.start()
            pending.append(c)
            src += seg.outs

    def both(row, end, f, *args):
        if 0 <= row < end:
            f(row, *args)
            f(row + 1, *args)

    flip(2)
    flip(4)
    both(2, rows + 4, volume, True)
    flip(0)
    both(0, rows + 4, volume, True)
    both(2, rows + 4, volume, False)
    both(0, rows + 4, volume, False)
    for row in range(0, rows + 6, 2):
        both(row + 4, rows + 4, volume, True)
        if row < rows + 2:
            hidden(row, 2)
        if 6 <= row < rows + 6:
            out(row - 6, 2)
        flip(row + 6)
        both(row + 4, rows + 4, volume, False)
        both(row - 2, rows + 2, hidden_spreads)
    for c in pending:
        c.wait()


def part_call(segments, ext, disp, rows, cols, chans, out_shape, operands):
    m_vol = sum(s.vol for s in segments)
    m_hid = sum(s.hid for s in segments)
    m_out = sum(s.outs for s in segments)
    pad = HALO if ext else 0
    span = max(128 * -(-s.vol // 128) + disp for s in segments)
    scratch = [
        pltpu.VMEM((len(segments), rows + 4, span, chans), BF),
        pltpu.VMEM((rows + 4, disp // 128, m_vol, 128), F32),
        pltpu.VMEM((rows + 4, m_hid, 3 * disp), BF),
        pltpu.VMEM((rows + 2, disp // 128, m_hid, 128), F32),
        pltpu.VMEM((rows + 2, m_out, 3 * disp), BF),
        pltpu.VMEM((rows, m_out, disp), BF),
        pltpu.SemaphoreType.DMA((rows, len(segments))),
    ]
    vmem, anywhere = pl.BlockSpec(memory_space=pltpu.VMEM), pl.BlockSpec(memory_space=pl.ANY)
    smem = pl.BlockSpec(memory_space=pltpu.SMEM)
    flops = 2 * 9 * disp * disp * ((rows + 2) * m_hid + rows * m_out)
    return pl.pallas_call(
        functools.partial(part_kernel, segments, ext, disp),
        out_shape=out_shape,
        in_specs=([smem] + [vmem] * (8 if ext else 4)
                  + [vmem, vmem] + ([anywhere] if ext else [])),
        out_specs=anywhere,
        scratch_shapes=scratch,
        input_output_aliases={len(operands) - 1: 0} if ext else {},
        compiler_params=pltpu.CompilerParams(vmem_limit_bytes=44 << 20),
        cost_estimate=pl.CostEstimate(flops=flops, bytes_accessed=6 << 20, transcendentals=0),
    )(*operands)


def pair_permute(x, axis, first):
    n = lax.axis_size(axis)
    perm = []
    for i in range(first, n - 1, 2):
        perm += [(i, i + 1), (i + 1, i)]
    return lax.ppermute(x, axis, perm)


def copy_all(copies, sems):
    copies = [pltpu.make_async_copy(src, dst, sems.at[i]) for i, (src, dst) in enumerate(copies)]
    for c in copies:
        c.start()
    for c in copies:
        c.wait()


def pack_kernel(flags, l_any, r_any, zl, a, b, zr, zl_buf, a_buf, b_buf, zr_buf, in_sems, out_sems):
    rows, cols, _ = l_any.shape
    wide = zl.shape[1] - HALO
    half = rows // 2
    fills = {
        0: [(r_any.at[pl.ds(0, half), pl.ds(cols - wide, wide)], zl_buf.at[pl.ds(0, half), pl.ds(0, wide)]),
                 (r_any.at[pl.ds(half, rows - half), pl.ds(cols - wide, wide)],
                  zl_buf.at[pl.ds(half, rows - half), pl.ds(0, wide)]),
                 (l_any.at[:, pl.ds(cols - HALO, HALO)], zl_buf.at[:, pl.ds(wide, HALO)])],
        3: [(r_any.at[:, pl.ds(0, HALO)], zr_buf.at[:, pl.ds(0, HALO)]),
                 (l_any.at[:, pl.ds(0, HALO)], zr_buf.at[:, pl.ds(HALO, HALO)])],
    }
    for i, buf, at in ((1, b_buf, flags[6]), (2, a_buf, flags[5])):
        fills[i] = [(l_any.at[pl.ds(at, 2)], buf.at[:, pl.ds(0, cols)]),
                      (r_any.at[pl.ds(at, 2)], buf.at[:, pl.ds(cols, cols)])]
    order = ((zl_buf, zl), (b_buf, b), (a_buf, a), (zr_buf, zr))
    started = []
    for i, (buf, _) in enumerate(order):
        started.append([pltpu.make_async_copy(src, dst, in_sems.at[i, j]) for j, (src, dst) in enumerate(fills[i])])
        for c in started[-1]:
            c.start()
    sends = []
    for i, (buf, msg) in enumerate(order):
        for c in started[i]:
            c.wait()
        sends.append(pltpu.make_async_copy(buf, msg, out_sems.at[i]))
        sends[-1].start()
    for c in sends:
        c.wait()


def pack(flags, left, right, disp):
    rows, cols, chans = left.shape
    anywhere = pl.BlockSpec(memory_space=pl.ANY)
    shapes = [(rows, disp + 2 * HALO, chans), (2, 2 * cols, chans), (2, 2 * cols, chans), (rows, 2 * HALO, chans)]
    return pl.pallas_call(
        pack_kernel,
        out_shape=[jax.ShapeDtypeStruct(s, BF) for s in shapes],
        in_specs=[pl.BlockSpec(memory_space=pltpu.SMEM), anywhere, anywhere],
        out_specs=[anywhere] * 4,
        scratch_shapes=[pltpu.VMEM(s, BF) for s in shapes]
        + [pltpu.SemaphoreType.DMA((4, 3)), pltpu.SemaphoreType.DMA((4,))],
        compiler_params=pltpu.CompilerParams(vmem_limit_bytes=PACK << 20),
        cost_estimate=pl.CostEstimate(flops=8 << 30, bytes_accessed=1 << 10, transcendentals=0),
    )(flags, left, right)


def pack_corners_kernel(flags, zl, zr, ca, cb, sems):
    wide = zl.shape[1]
    copies = []
    for msg, at in ((cb, flags[6]), (ca, flags[5])):
        copies.append((zl.at[pl.ds(at, 2)], msg.at[:, pl.ds(0, wide)]))
        copies.append((zr.at[pl.ds(at, 2)], msg.at[:, pl.ds(wide, 2 * HALO)]))
    copy_all(copies, sems)


def pack_corners(flags, zl, zr):
    anywhere = pl.BlockSpec(memory_space=pl.ANY)
    shape = jax.ShapeDtypeStruct((2, zl.shape[1] + zr.shape[1], zl.shape[2]), BF)
    return pl.pallas_call(
        pack_corners_kernel,
        out_shape=[shape, shape],
        in_specs=[pl.BlockSpec(memory_space=pltpu.SMEM)] + [anywhere] * 2,
        out_specs=[anywhere] * 2,
        scratch_shapes=[pltpu.SemaphoreType.DMA((4,))],
        compiler_params=pltpu.CompilerParams(vmem_limit_bytes=1 << 20),
        cost_estimate=pl.CostEstimate(flops=8 << 30, bytes_accessed=1 << 10, transcendentals=0),
    )(flags, zl, zr)


def local(left, right, conv_first, conv_second):
    rows, cols, chans = left.shape
    disp = conv_first.shape[2]
    n_row, n_col = lax.axis_size("row"), lax.axis_size("col")
    ri, ci = lax.axis_index("row"), lax.axis_index("col")
    odd = ri % 2
    a_at = jnp.where(odd == 1, 0, rows - 2)
    b_at = jnp.where(odd == 1, rows - 2, 0)
    flags = jnp.stack([odd, ri > 0, ri < n_row - 1, ci > 0, ci < n_col - 1, a_at, b_at]).astype(jnp.int32)
    k1 = conv_first.reshape(9 * disp, disp)
    k2 = conv_second.reshape(9 * disp, disp)

    zl_msg, a_msg, b_msg, zr_msg = pack(flags, left, right, disp)
    zl = lax.ppermute(zl_msg, "col", [(i, i + 1) for i in range(n_col - 1)])
    b = pair_permute(b_msg, "row", 1)
    a = pair_permute(a_msg, "row", 0)
    zr = lax.ppermute(zr_msg, "col", [(i + 1, i) for i in range(n_col - 1)])

    out_shape = jax.ShapeDtypeStruct((rows, cols, disp), BF)
    mid = [Segment(disp, cols - disp - 2 * HALO)]
    out = part_call(mid, False, disp, rows, cols, chans, out_shape, (flags, left, right, a, b, k1, k2))

    ca_msg, cb_msg = pack_corners(flags, zl, zr)
    cb = pair_permute(cb_msg, "row", 1)
    ca = pair_permute(ca_msg, "row", 0)
    rest = [Segment(-HALO, disp + HALO), Segment(cols - 2 * HALO, HALO)]
    return part_call(rest, True, disp, rows, cols, chans, out_shape,
                     (flags, left, right, a, b, zl, zr, ca, cb, k1, k2, out))


def solution(mesh):
    spec = P(("strip", "row"), "col", None)
    return jax.shard_map(local, mesh=mesh, in_specs=(spec, spec, P(), P()), out_specs=spec, check_vma=False)
```

```python
import functools

import jax
import jax.numpy as jnp
from jax import lax
from jax.experimental import pallas as pl
from jax.experimental.pallas import tpu as pltpu
from jax.sharding import PartitionSpec as P

BF = jnp.bfloat16
F32 = jnp.float32
HALO = 16
PACK = 58


class Segment:
    def __init__(self, base, outs):
        self.base, self.outs = base, outs
        self.hid = outs + 16
        self.vol = outs + 32


def part_kernel(segments, ext, disp, *refs):
    refs = list(refs)
    flags, l_own, r_own, b_ref, a_ref = refs[:5]
    zl, zr, ca, cb = refs[5:9] if ext else (None,) * 4
    k1, k2 = refs[9:11] if ext else refs[5:7]
    out_any, (rrev, vf, vs, hf, hs, obuf, osems) = refs[-9 if not ext else -8], refs[-7:]
    rows, cols, chans = l_own.shape
    pad = HALO if ext else 0
    lpad = disp + HALO if ext else 0
    scale = 1.0 / (chans ** 0.5)
    odd = flags[0].astype(F32)

    def pieces(row, lo, n, right, own, left_edge, right_edge):
        out = []
        if lo < 0:
            m = min(n, -lo)
            at = left_edge[1] + lo + lpad if right else left_edge[1] + lpad + pad + lo
            out.append(left_edge[0][row, at:at + m, :])
            lo, n = lo + m, n - m
        if n and lo < cols:
            m = min(n, cols - lo)
            out.append(own[0][row, own[1] + lo:own[1] + lo + m, :])
            lo, n = lo + m, n - m
        if n:
            at = right_edge[1] + lo - cols + (0 if right else pad)
            out.append(right_edge[0][row, at:at + n, :])
        return out[0] if len(out) == 1 else jnp.concatenate(out, axis=0)

    def columns(row, lo, n, right):
        if 2 <= row < rows + 2:
            return pieces(row - 2, lo, n, right, (r_own if right else l_own, 0), (zl, 0), (zr, 0))
        at, share = (row, odd) if row < 2 else (row - rows - 2, 1.0 - odd)
        start = cols if right else 0
        one = pieces(at, lo, n, right, (a_ref, start), (ca, 0), (ca, lpad + pad))
        two = pieces(at, lo, n, right, (b_ref, start), (cb, 0), (cb, lpad + pad))
        return (one.astype(F32) * share + two.astype(F32) * (1.0 - share)).astype(BF)

    mirror = 7 - lax.broadcasted_iota(jnp.int32, (8, 128), 0)

    def flip(row):
        def unit(s, seg, t):
            span = 128 * -(-seg.vol // 128) + disp
            start = seg.base - disp + 128 * t
            n = min(128, seg.vol + disp - 128 * t)
            both = jnp.concatenate([columns(row + q, start, n, True) for q in range(2)], axis=1)
            wide = both.astype(F32)
            res = jnp.concatenate([jnp.concatenate([
                jnp.take_along_axis(wide[n - 8 * (i + 1):n - 8 * i, chans * q:chans * (q + 1)], mirror, axis=0,
                                    mode="promise_in_bounds") for q in range(2)], axis=1)
                for i in range(n // 8)], axis=0).astype(BF)
            for q in range(2):
                rrev[s, row + q, span - 128 * t - n:span - 128 * t, :] = res[:, chans * q:chans * (q + 1)]

        if row < rows + 4:
            for s, seg in enumerate(segments):
                for t in range(-(-(seg.vol + disp) // 128)):
                    unit(s, seg, t)

    def volume(row, scores_now):
        slot = row

        def score(s, seg, dst, b):
            n = min(128, seg.vol - 128 * b)
            u = 128 * (-(-seg.vol // 128) - 1 - b)
            left = columns(row, seg.base + 128 * b, n, False)
            scores = lax.dot_general(left, rrev[s, slot, u:u + 128 + disp, :], (((1,), (1,)), ((), ())),
                                     preferred_element_type=F32) * scale
            rolled = pltpu.roll(scores, 1, 1, stride=1, stride_axis=0)
            for h in range(disp // 128):
                vf[slot, h, dst + 128 * b:dst + 128 * b + n, :] = rolled[:, 128 * (h + 1):128 * (h + 2)]

        def spread(b):
            src, dst = 0, 0
            for seg in segments:
                for h in range(disp // 128):
                    vs[row, dst:dst + seg.hid, disp * b + 128 * h:disp * b + 128 * (h + 1)] = (
                        vf[slot, h, pl.ds(src + 14 + b, seg.hid), :].astype(BF))
                src += seg.vol
                dst += seg.hid

        dst = 0
        if scores_now:
            for s, seg in enumerate(segments):
                for b in range(-(-seg.vol // 128)):
                    score(s, seg, dst, b)
                dst += seg.vol
        else:
            for b in range(3):
                spread(b)

    def conv(src, row, count, kernel):
        x = jnp.concatenate([src[row + a:row + a + count].reshape(count * src.shape[1], src.shape[2])
                             for a in range(3)], axis=1)
        res = jnp.maximum(jnp.dot(x, kernel[...], preferred_element_type=F32), 0.0)
        return [res[q * src.shape[1]:(q + 1) * src.shape[1]] for q in range(count)]

    m_hid = sum(seg.hid for seg in segments)
    m_out = sum(seg.outs for seg in segments)

    def hidden(row, count):
        for q, one in enumerate(conv(vs, row, count, k1)):
            if row + q == 0:
                one = one * flags[1].astype(F32)
            if row + q == rows + 1:
                one = one * flags[2].astype(F32)
            for h in range(disp // 128):
                hf[row + q, h] = one[:, 128 * h:128 * (h + 1)]

    def hidden_spreads(row):
        slot = row

        def spread(b):
            src, dst = 0, 0
            for seg in segments:
                for edge, flag in ((-1, flags[3]), (cols, flags[4])):
                    pos = edge - (seg.base + 15)
                    if b == 0 and 0 <= pos < seg.outs + 2:
                        at = src + pos // 8 * 8
                        keep = lax.broadcasted_iota(jnp.int32, (8, 128), 0) != pos % 8
                        keep = jnp.where(keep, 1.0, flag.astype(F32))
                        for h in range(disp // 128):
                            hf[slot, h, at:at + 8, :] = hf[slot, h, at:at + 8, :] * keep
                for h in range(disp // 128):
                    hs[row, dst:dst + seg.outs, disp * b + 128 * h:disp * b + 128 * (h + 1)] = (
                        hf[slot, h, pl.ds(src + b, seg.outs), :].astype(BF))
                src += seg.hid
                dst += seg.outs

        for b in range(3):
            spread(b)

    pending = []

    def out(row, count):
        for q, one in enumerate(conv(hs, row, count, k2)):
            obuf[row + q] = one.astype(BF)
        src = 0
        for s, seg in enumerate(segments):
            c = pltpu.make_async_copy(
                obuf.at[pl.ds(row, count), pl.ds(src, seg.outs)],
                out_any.at[pl.ds(row, count), pl.ds(seg.base + 16, seg.outs)], osems.at[row, s])
            c.start()
            pending.append(c)
            src += seg.outs

    def both(row, end, f, *args):
        if 0 <= row < end:
            f(row, *args)
            f(row + 1, *args)

    flip(2)
    flip(4)
    both(2, rows + 4, volume, True)
    flip(0)
    both(0, rows + 4, volume, True)
    both(2, rows + 4, volume, False)
    both(0, rows + 4, volume, False)
    for row in range(0, rows + 6, 2):
        both(row + 4, rows + 4, volume, True)
        if row < rows + 2:
            hidden(row, 2)
        if 6 <= row < rows + 6:
            out(row - 6, 2)
        flip(row + 6)
        both(row + 4, rows + 4, volume, False)
        both(row - 2, rows + 2, hidden_spreads)
    for c in pending:
        c.wait()


def part_call(segments, ext, disp, rows, cols, chans, out_shape, operands):
    m_vol = sum(s.vol for s in segments)
    m_hid = sum(s.hid for s in segments)
    m_out = sum(s.outs for s in segments)
    pad = HALO if ext else 0
    span = max(128 * -(-s.vol // 128) + disp for s in segments)
    scratch = [
        pltpu.VMEM((len(segments), rows + 4, span, chans), BF),
        pltpu.VMEM((rows + 4, disp // 128, m_vol, 128), F32),
        pltpu.VMEM((rows + 4, m_hid, 3 * disp), BF),
        pltpu.VMEM((rows + 2, disp // 128, m_hid, 128), F32),
        pltpu.VMEM((rows + 2, m_out, 3 * disp), BF),
        pltpu.VMEM((rows, m_out, disp), BF),
        pltpu.SemaphoreType.DMA((rows, len(segments))),
    ]
    vmem, anywhere = pl.BlockSpec(memory_space=pltpu.VMEM), pl.BlockSpec(memory_space=pl.ANY)
    smem = pl.BlockSpec(memory_space=pltpu.SMEM)
    flops = 2 * 9 * disp * disp * ((rows + 2) * m_hid + rows * m_out)
    return pl.pallas_call(
        functools.partial(part_kernel, segments, ext, disp),
        out_shape=out_shape if ext else [out_shape, jax.ShapeDtypeStruct((16, 128), BF)],
        in_specs=([smem] + [vmem] * (8 if ext else 4)
                  + [vmem, vmem] + ([anywhere] if ext else [])),
        out_specs=anywhere if ext else [anywhere, anywhere],
        scratch_shapes=scratch,
        input_output_aliases={len(operands) - 1: 0} if ext else {},
        compiler_params=pltpu.CompilerParams(vmem_limit_bytes=44 << 20),
        cost_estimate=pl.CostEstimate(flops=flops, bytes_accessed=6 << 20, transcendentals=0),
    )(*operands)


def pair_permute(x, axis, first):
    n = lax.axis_size(axis)
    perm = []
    for i in range(first, n - 1, 2):
        perm += [(i, i + 1), (i + 1, i)]
    return lax.ppermute(x, axis, perm)


def copy_all(copies, sems):
    copies = [pltpu.make_async_copy(src, dst, sems.at[i]) for i, (src, dst) in enumerate(copies)]
    for c in copies:
        c.start()
    for c in copies:
        c.wait()


def pack_kernel(flags, l_any, r_any, zl, a, b, zr, zl_buf, a_buf, b_buf, zr_buf, in_sems, out_sems):
    rows, cols, _ = l_any.shape
    wide = zl.shape[1] - HALO
    half = rows // 2
    fills = {
        0: [(r_any.at[pl.ds(0, half), pl.ds(cols - wide, wide)], zl_buf.at[pl.ds(0, half), pl.ds(0, wide)]),
                 (r_any.at[pl.ds(half, rows - half), pl.ds(cols - wide, wide)],
                  zl_buf.at[pl.ds(half, rows - half), pl.ds(0, wide)]),
                 (l_any.at[:, pl.ds(cols - HALO, HALO)], zl_buf.at[:, pl.ds(wide, HALO)])],
        3: [(r_any.at[:, pl.ds(0, HALO)], zr_buf.at[:, pl.ds(0, HALO)]),
                 (l_any.at[:, pl.ds(0, HALO)], zr_buf.at[:, pl.ds(HALO, HALO)])],
    }
    for i, buf, at in ((1, b_buf, flags[6]), (2, a_buf, flags[5])):
        fills[i] = [(l_any.at[pl.ds(at, 2)], buf.at[:, pl.ds(0, cols)]),
                      (r_any.at[pl.ds(at, 2)], buf.at[:, pl.ds(cols, cols)])]
    order = ((zl_buf, zl), (b_buf, b), (a_buf, a), (zr_buf, zr))
    started = []
    for i, (buf, _) in enumerate(order):
        started.append([pltpu.make_async_copy(src, dst, in_sems.at[i, j]) for j, (src, dst) in enumerate(fills[i])])
        for c in started[-1]:
            c.start()
    sends = []
    for i, (buf, msg) in enumerate(order):
        for c in started[i]:
            c.wait()
        sends.append(pltpu.make_async_copy(buf, msg, out_sems.at[i]))
        sends[-1].start()
    for c in sends:
        c.wait()


def pack(flags, left, right, disp):
    rows, cols, chans = left.shape
    anywhere = pl.BlockSpec(memory_space=pl.ANY)
    shapes = [(rows, disp + 2 * HALO, chans), (2, 2 * cols, chans), (2, 2 * cols, chans), (rows, 2 * HALO, chans)]
    return pl.pallas_call(
        pack_kernel,
        out_shape=[jax.ShapeDtypeStruct(s, BF) for s in shapes],
        in_specs=[pl.BlockSpec(memory_space=pltpu.SMEM), anywhere, anywhere],
        out_specs=[anywhere] * 4,
        scratch_shapes=[pltpu.VMEM(s, BF) for s in shapes]
        + [pltpu.SemaphoreType.DMA((4, 3)), pltpu.SemaphoreType.DMA((4,))],
        compiler_params=pltpu.CompilerParams(vmem_limit_bytes=PACK << 20),
        cost_estimate=pl.CostEstimate(flops=8 << 30, bytes_accessed=1 << 10, transcendentals=0),
    )(flags, left, right)


def pack_corners_kernel(flags, zl, zr, _, ca, cb, sems):
    wide = zl.shape[1]
    copies = []
    for msg, at in ((cb, flags[6]), (ca, flags[5])):
        copies.append((zl.at[pl.ds(at, 2)], msg.at[:, pl.ds(0, wide)]))
        copies.append((zr.at[pl.ds(at, 2)], msg.at[:, pl.ds(wide, 2 * HALO)]))
    copy_all(copies, sems)


def pack_corners(flags, zl, zr, after):
    anywhere = pl.BlockSpec(memory_space=pl.ANY)
    shape = jax.ShapeDtypeStruct((2, zl.shape[1] + zr.shape[1], zl.shape[2]), BF)
    return pl.pallas_call(
        pack_corners_kernel,
        out_shape=[shape, shape],
        in_specs=[pl.BlockSpec(memory_space=pltpu.SMEM)] + [anywhere] * 3,
        out_specs=[anywhere] * 2,
        scratch_shapes=[pltpu.SemaphoreType.DMA((4,))],
        compiler_params=pltpu.CompilerParams(vmem_limit_bytes=1 << 20),
        cost_estimate=pl.CostEstimate(flops=8 << 30, bytes_accessed=1 << 10, transcendentals=0),
    )(flags, zl, zr, after)


def local(left, right, conv_first, conv_second):
    rows, cols, chans = left.shape
    disp = conv_first.shape[2]
    n_row, n_col = lax.axis_size("row"), lax.axis_size("col")
    ri, ci = lax.axis_index("row"), lax.axis_index("col")
    odd = ri % 2
    a_at = jnp.where(odd == 1, 0, rows - 2)
    b_at = jnp.where(odd == 1, rows - 2, 0)
    flags = jnp.stack([odd, ri > 0, ri < n_row - 1, ci > 0, ci < n_col - 1, a_at, b_at]).astype(jnp.int32)
    k1 = conv_first.reshape(9 * disp, disp)
    k2 = conv_second.reshape(9 * disp, disp)

    zl_msg, a_msg, b_msg, zr_msg = pack(flags, left, right, disp)
    zl = lax.ppermute(zl_msg, "col", [(i, i + 1) for i in range(n_col - 1)])
    b = pair_permute(b_msg, "row", 1)
    a = pair_permute(a_msg, "row", 0)
    zr = lax.ppermute(zr_msg, "col", [(i + 1, i) for i in range(n_col - 1)])

    out_shape = jax.ShapeDtypeStruct((rows, cols, disp), BF)
    mid = [Segment(disp, cols - disp - 2 * HALO)]
    out, after = part_call(mid, False, disp, rows, cols, chans, out_shape, (flags, left, right, b, a, k1, k2))

    ca_msg, cb_msg = pack_corners(flags, zl, zr, after)
    cb = pair_permute(cb_msg, "row", 1)
    ca = pair_permute(ca_msg, "row", 0)
    rest = [Segment(-HALO, disp + HALO), Segment(cols - 2 * HALO, HALO)]
    return part_call(rest, True, disp, rows, cols, chans, out_shape,
                     (flags, left, right, b, a, zl, zr, ca, cb, k1, k2, out))


def solution(mesh):
    spec = P(("strip", "row"), "col", None)
    return jax.shard_map(local, mesh=mesh, in_specs=(spec, spec, P(), P()), out_specs=spec, check_vma=False)
```
